256 devices in a mesh: dp: 64 (over x, z, core), rep: 4 (over y).
Axes of the slice: x: 4, y: 4, z: 8, core: 2. Of those that a mesh axis runs over, the one named last changes fastest.
Arguments:
- query_hidden: bfloat16 [512, 32, 768], P(('dp', 'rep')), may hold values from -6 to 6
- passage_hidden: bfloat16 [2048, 180, 768], P(('dp', 'rep')), may hold values from -6 to 6
- projection: bfloat16 [768, 128], replicated, may hold values from -0.21875 to 0.21875
- negatives: int32 [512, 128], P(('dp', 'rep')), may hold values from 0 to 2047, as said below
- positions: int32 [512, 128, 32], P(('dp', 'rep')), may hold values from 0 to 179
- teacher: float32 [512, 128], P(('dp', 'rep')), may hold values from -8 to 8
Outputs:
- grad_passages: bfloat16 [2048, 180, 128], P(('dp', 'rep'))
- grad_projection: float32 [768, 128], replicated
The draws below stay inside these ranges and needn't reach their ends.
Inputs may be any that keep to these rules, and one draw needn't show every extreme that they name: `negatives`: queries and passages lie in blocks of 2 queries and 8 passages per device of dp+rep, device number dp index * (size of rep) + rep index. Every listed passage belongs to a device with the same rep index as the query's and another dp index. Of the 256 pairs of one device, every other dp index owns the passages of at most 5 pairs, and some dp index owns exactly 5.
All inputs are finite; a program needn't handle non-finite values.
Results may differ from the reference program's by a relative error of at most 0.015.
Values may be sent and summed in bfloat16 or wider, within the bound.
No kernel may reach another device: no remote copies, remote signals or barrier semaphores. Data moves between devices by JAX's collectives and lax.ppermute only.
A program may use at most 64 MiB of HBM per device.

```python
import math
import jax
import jax.numpy as jnp
from jax import lax

D_HID = 768
E = 128
LQ = 32
LP = 180
NEG = 128
QD = 2
PD = 8
QUERIES = 512
PASSAGES = 2048
CAP = 5
N_DP = 64
N_REP = 4


def draw_negatives(key, part):
    key = jax.random.fold_in(key, 11)
    pair_count = QD * NEG

    def one_device(device_id):
        device_key = jax.random.fold_in(key, device_id)
        round_keys = jax.random.split(jax.random.fold_in(device_key, 1), CAP)
        round_perms = jax.vmap(lambda round_key: jax.random.permutation(round_key, N_DP - 1))(round_keys) + 1
        offsets = jax.random.permutation(jax.random.fold_in(device_key, 2), round_perms.reshape(-1)[:pair_count])
        within = jax.random.randint(jax.random.fold_in(device_key, 3), (pair_count,), 0, PD)
        dp_index = device_id // N_REP
        rep_index = device_id % N_REP
        owner_dp = (dp_index + offsets) % N_DP
        return ((owner_dp * N_REP + rep_index) * PD + within).reshape(QD, NEG)
    passage_ids = jax.vmap(one_device)(jnp.arange(N_DP * N_REP, dtype=jnp.int32))
    return passage_ids.reshape(QD * N_DP * N_REP, NEG).astype(jnp.int32)


def place_ends(array, rng, smallest, largest):
    index_at = [jax.random.randint(jax.random.fold_in(rng, axis), (), 0, length) for axis, length in enumerate(array.shape)]
    widest = array.shape.index(max(array.shape))
    next_to = index_at[:widest] + [(index_at[widest] + 1) % array.shape[widest]] + index_at[widest + 1:]
    return array.at[tuple(index_at)].set(smallest).at[tuple(next_to)].set(largest)


def block_scale(own_key, shape, pieces, smallest, largest):
    gain = 1.0
    for dim, shards_of in pieces:
        draws = jax.random.uniform(jax.random.fold_in(jax.random.fold_in(own_key, 6), dim), (shards_of,), jnp.float32, smallest / len(pieces), largest / len(pieces))
        gain = gain * jnp.repeat(jnp.exp(draws), shape[dim] // shards_of).reshape((-1,) + (1,) * (len(shape) - 1 - dim))
    return gain


def bell_draw(stream_key, shape, scale, bound, pieces=(), kind=jnp.bfloat16):
    level = block_scale(stream_key, shape, pieces, -0.22, 0.18) if pieces else 1.0
    drawn = jax.random.normal(stream_key, shape, jnp.float32) * scale * level
    return jnp.minimum(jnp.maximum(drawn, -bound), bound).astype(kind)


def setup_inputs(seed: int = 0) -> dict:
    keys = jax.random.split(jax.random.key(seed), 7)
    query_hidden = bell_draw(keys[0], (QUERIES, LQ, D_HID), 1.0, 6.0, ((0, 256),))
    passage_hidden = bell_draw(keys[1], (PASSAGES, LP, D_HID), 1.0, 6.0, ((0, 256),))
    projection = bell_draw(keys[2], (D_HID, E), D_HID ** -0.5, 0.21875)
    negatives = draw_negatives(jax.random.fold_in(keys[6], 71), 0)
    positions = place_ends(jax.random.randint(keys[4], (QUERIES, NEG, LQ), 0, LP), jax.random.fold_in(keys[4], 1), 0, LP - 1).astype(jnp.int32)
    teacher = bell_draw(keys[5], (QUERIES, NEG), 2.0, 8.0, ((0, 256),), jnp.float32)
    return dict(query_hidden=query_hidden, passage_hidden=passage_hidden, projection=projection, negatives=negatives, positions=positions, teacher=teacher)


def unit_rows(raw):
    length = jnp.sqrt(lax.optimization_barrier(jnp.sum(raw * raw, axis=-1, keepdims=True)) + 1e-06)
    return (raw / length, length)

def unit_back(grad, unit, length):
    return (grad - unit * lax.optimization_barrier(jnp.sum(unit * grad, axis=-1, keepdims=True))) / length

def pair_weights(scores, teacher):
    student = jnp.exp(scores)
    student = student / lax.optimization_barrier(jnp.sum(student, axis=-1, keepdims=True))
    target = jnp.exp(teacher)
    target = target / lax.optimization_barrier(jnp.sum(target, axis=-1, keepdims=True))
    return (scores.shape[-1] * (student - target)).astype(jnp.bfloat16)

def reference(query_hidden, passage_hidden, projection, negatives, positions, teacher):
    query_flat = query_hidden.reshape(-1, D_HID)
    passage_flat = passage_hidden.reshape(-1, D_HID)
    query_unit, query_length = unit_rows(jnp.dot(query_flat, projection, preferred_element_type=jnp.float32))
    query_emb = query_unit.astype(jnp.bfloat16).reshape(-1, LQ, E)
    passage_unit, passage_length = unit_rows(jnp.dot(passage_flat, projection, preferred_element_type=jnp.float32))
    passage_emb = passage_unit.astype(jnp.bfloat16)
    block_count = query_emb.shape[0] // QD

    def one_block(carry, block):
        embedded, neg_ids, picks, teach = block
        token_rows = (neg_ids[:, :, None] * LP + picks).reshape(-1)
        tokens = passage_emb[token_rows].reshape(QD, NEG, LQ, E)
        scores = jnp.einsum('qnie,qie->qn', tokens.astype(jnp.float32), embedded.astype(jnp.float32))
        weights = pair_weights(scores, teach)
        query_grad = jnp.einsum('qn,qnie->qie', weights.astype(jnp.float32), tokens.astype(jnp.float32))
        token_grad = (weights.astype(jnp.float32)[:, :, None, None] * embedded.astype(jnp.float32)[:, None]).astype(jnp.bfloat16)
        carry = carry.at[token_rows].add(token_grad.reshape(-1, E).astype(jnp.float32))
        return (carry, query_grad)
    blocks = (query_emb.reshape(block_count, QD, LQ, E), negatives.reshape(block_count, QD, NEG), positions.reshape(block_count, QD, NEG, LQ), teacher.reshape(block_count, QD, NEG))
    start = jnp.zeros((passage_emb.shape[0], E), jnp.float32)
    passage_grad, query_grad = lax.scan(one_block, start, blocks)
    query_raw_grad = unit_back(query_grad.reshape(-1, E), query_unit, query_length).astype(jnp.bfloat16)
    passage_raw_grad = unit_back(passage_grad, passage_unit, passage_length).astype(jnp.bfloat16)
    total = jnp.dot(query_flat.T, query_raw_grad, preferred_element_type=jnp.float32)
    total = total + jnp.dot(passage_flat.T, passage_raw_grad, preferred_element_type=jnp.float32)
    scale = 1.0 / math.sqrt(query_flat.shape[0] + passage_flat.shape[0])
    return (passage_raw_grad.reshape(-1, LP, E), total * scale)
```

```python
import math

import jax
import jax.numpy as jnp
from jax import lax
from jax.sharding import PartitionSpec as P

slot_block = 64


def unit_rows(raw):
    length = jnp.sqrt(jnp.sum(raw * raw, axis=-1, keepdims=True) + 1e-06)
    return (raw / length, length)


def unit_back(grad, unit, length):
    return (grad - unit * jnp.sum(unit * grad, axis=-1, keepdims=True)) / length


def pair_weights(scores, teacher):
    student = jnp.exp(scores)
    student = student / jnp.sum(student, axis=-1, keepdims=True)
    target = jnp.exp(teacher)
    target = target / jnp.sum(target, axis=-1, keepdims=True)
    return (scores.shape[-1] * (student - target)).astype(jnp.bfloat16)


def padded_blocks(within, picks):
    slot_total = within.shape[0]
    block_count = (slot_total + slot_block - 1) // slot_block
    extra = block_count * slot_block - slot_total
    within_pad = within.reshape(block_count, slot_block)
    picks_pad = picks.reshape(block_count, slot_block, picks.shape[1])
    return (within_pad, picks_pad, extra)


def select_tokens(passage_emb, pass_count, pass_len, within, picks):
    emb_dim = passage_emb.shape[1]
    slot_total = within.shape[0]
    whole_rows = passage_emb.reshape(pass_count, pass_len * emb_dim)
    within_pad, picks_pad, extra = padded_blocks(within, picks)

    def pick_block(block):
        block_within, block_picks = block
        which = (block_within[:, None] == jnp.arange(pass_count, dtype=jnp.int32)[None, :]).astype(
            jnp.bfloat16
        )
        chosen = jnp.dot(which, whole_rows, preferred_element_type=jnp.float32).astype(jnp.bfloat16)
        chosen = chosen.reshape(slot_block, pass_len, emb_dim)
        where = (
            block_picks[:, :, None] == jnp.arange(pass_len, dtype=jnp.int32)[None, None, :]
        ).astype(jnp.bfloat16)
        return jnp.einsum("bip,bpe->bie", where, chosen, preferred_element_type=jnp.float32).astype(
            jnp.bfloat16
        )

    picked = lax.map(pick_block, (within_pad, picks_pad))
    return picked.reshape(-1, picks.shape[1], emb_dim)


def spread_grads(grads, pass_count, pass_len, within, picks):
    emb_dim = grads.shape[2]
    query_len = grads.shape[1]
    within_pad, picks_pad, extra = padded_blocks(within, picks)
    grads_pad = grads.reshape(-1, slot_block, query_len, emb_dim)

    def add_block(total, block):
        block_within, block_picks, block_grads = block
        where = (
            block_picks[:, :, None] == jnp.arange(pass_len, dtype=jnp.int32)[None, None, :]
        ).astype(jnp.bfloat16)
        placed = jnp.einsum("bip,bie->bpe", where, block_grads, preferred_element_type=jnp.float32)
        which = (block_within[:, None] == jnp.arange(pass_count, dtype=jnp.int32)[None, :]).astype(
            jnp.float32
        )
        total = total + jnp.dot(
            which.T, placed.reshape(slot_block, pass_len * emb_dim), precision=lax.Precision.HIGHEST
        )
        return (total, None)

    start = jnp.zeros((pass_count, pass_len * emb_dim), jnp.float32)
    total, _ = lax.scan(add_block, start, (within_pad, picks_pad, grads_pad))
    return total.reshape(pass_count * pass_len, emb_dim)


def reduce_all(term):
    owners = lax.axis_size("dp")
    reps = lax.axis_size("rep")
    rows, cols = term.shape
    pieces = term.astype(jnp.bfloat16).reshape(owners, rows // owners, cols)
    pieces = lax.all_to_all(pieces, "dp", split_axis=0, concat_axis=0, tiled=True)
    mine = jnp.sum(pieces.astype(jnp.float32), axis=0)
    copies = jnp.broadcast_to(mine[None], (reps,) + mine.shape)
    copies = lax.all_to_all(copies, "rep", split_axis=0, concat_axis=0, tiled=True)
    mine = jnp.sum(copies, axis=0).astype(jnp.bfloat16)
    copies = jnp.broadcast_to(mine[None], (owners,) + mine.shape)
    copies = lax.all_to_all(copies, "dp", split_axis=0, concat_axis=0, tiled=True)
    return copies.reshape(rows, cols).astype(jnp.float32)


def per_device(query_hidden, passage_hidden, projection, negatives, positions, teacher):
    query_count, query_len, hidden_dim = query_hidden.shape
    pass_count, pass_len, _ = passage_hidden.shape
    emb_dim = projection.shape[1]
    neg_count = negatives.shape[1]
    owners = lax.axis_size("dp")
    rep_count = lax.axis_size("rep")
    pair_count = query_count * neg_count
    capacity = (pair_count + owners - 2) // (owners - 1)
    slot_total = owners * capacity
    query_flat = query_hidden.reshape(-1, hidden_dim)
    passage_flat = passage_hidden.reshape(-1, hidden_dim)
    query_unit, query_length = unit_rows(
        jnp.dot(query_flat, projection, preferred_element_type=jnp.float32)
    )
    query_emb = query_unit.astype(jnp.bfloat16).reshape(query_count, query_len, emb_dim)
    passage_unit, passage_length = unit_rows(
        jnp.dot(passage_flat, projection, preferred_element_type=jnp.float32)
    )
    passage_emb = passage_unit.astype(jnp.bfloat16)
    flat_ids = negatives.reshape(-1)
    owner_of = flat_ids // (rep_count * pass_count)
    within = flat_ids % pass_count
    owner_table = (owner_of[:, None] == jnp.arange(owners, dtype=jnp.int32)[None, :]).astype(
        jnp.int32
    )
    slot_rank = jnp.sum((jnp.cumsum(owner_table, axis=0) - owner_table) * owner_table, axis=1)
    slot_index = owner_of * capacity + slot_rank
    query_slot = jnp.arange(pair_count, dtype=jnp.int32) // neg_count
    slot_match = slot_index[:, None] == jnp.arange(slot_total, dtype=jnp.int32)[None, :]
    slot_exact = slot_match.astype(jnp.float32)
    slot_table = slot_match.astype(jnp.bfloat16)
    request_fields = jnp.concatenate(
        [within[:, None], query_slot[:, None], positions.reshape(pair_count, query_len)], axis=1
    ).astype(jnp.float32)
    placed_fields = jnp.dot(slot_exact.T, request_fields, precision=lax.Precision.HIGHEST).astype(
        jnp.int32
    )
    request_meta = placed_fields[:, 0:2]
    request_pos = placed_fields[:, 2:]
    arrived_meta, arrived_pos = (
        lax.all_to_all(
            request_meta.reshape(owners, capacity, 2), "dp", split_axis=0, concat_axis=0, tiled=True
        ),
        lax.all_to_all(
            request_pos.reshape(owners, capacity, query_len),
            "dp",
            split_axis=0,
            concat_axis=0,
            tiled=True,
        ),
    )
    arrived_within = arrived_meta[:, :, 0].reshape(-1)
    arrived_picks = arrived_pos.reshape(slot_total, query_len)
    picked = select_tokens(passage_emb, pass_count, pass_len, arrived_within, arrived_picks)
    returned = lax.all_to_all(
        picked.reshape(owners, capacity, query_len, emb_dim),
        "dp",
        split_axis=0,
        concat_axis=0,
        tiled=True,
    )
    tokens = jnp.dot(
        slot_table,
        returned.reshape(slot_total, query_len * emb_dim),
        preferred_element_type=jnp.float32,
    ).astype(jnp.bfloat16)
    tokens = tokens.reshape(query_count, neg_count, query_len, emb_dim)
    scores = jnp.einsum("qnie,qie->qn", tokens, query_emb, preferred_element_type=jnp.float32)
    weights = pair_weights(scores, teacher)
    query_grad = jnp.einsum("qn,qnie->qie", weights, tokens, preferred_element_type=jnp.float32)
    token_grad = (
        weights.astype(jnp.float32)[:, :, None, None] * query_emb.astype(jnp.float32)[:, None]
    ).astype(jnp.bfloat16)
    outgoing = jnp.dot(
        slot_table.T,
        token_grad.reshape(pair_count, query_len * emb_dim),
        preferred_element_type=jnp.float32,
    ).astype(jnp.bfloat16)
    arrived_grad = lax.all_to_all(
        outgoing.reshape(owners, capacity, query_len, emb_dim),
        "dp",
        split_axis=0,
        concat_axis=0,
        tiled=True,
    )
    passage_grad = spread_grads(
        arrived_grad.reshape(slot_total, query_len, emb_dim),
        pass_count,
        pass_len,
        arrived_within,
        arrived_picks,
    )
    query_raw_grad = unit_back(query_grad.reshape(-1, emb_dim), query_unit, query_length).astype(
        jnp.bfloat16
    )
    passage_raw_grad = unit_back(passage_grad, passage_unit, passage_length).astype(jnp.bfloat16)
    local_sum = jnp.dot(query_flat.T, query_raw_grad, preferred_element_type=jnp.float32)
    local_sum = local_sum + jnp.dot(
        passage_flat.T, passage_raw_grad, preferred_element_type=jnp.float32
    )
    total = reduce_all(local_sum)
    scale = 1.0 / math.sqrt(owners * rep_count * (query_count * query_len + pass_count * pass_len))
    return (passage_raw_grad.reshape(pass_count, pass_len, emb_dim), total * scale)


def solution(mesh):
    in_specs = (
        P(("dp", "rep"), None, None),
        P(("dp", "rep"), None, None),
        P(),
        P(("dp", "rep"), None),
        P(("dp", "rep"), None, None),
        P(("dp", "rep"), None),
    )
    out_specs = (P(("dp", "rep"), None, None), P())
    return jax.shard_map(
        per_device, mesh=mesh, in_specs=in_specs, out_specs=out_specs, check_vma=False
    )
```

```python
import math

import jax
import jax.numpy as jnp
from jax import lax
from jax.experimental import pallas as pl
from jax.experimental.pallas import tpu as pltpu
from jax.sharding import PartitionSpec as P

F32 = jnp.float32
BF16 = jnp.bfloat16
SLOTS = 8
META_ROWS = 16
CODE, WHICH, VALID, HIGH, MID, LOW = 32, 33, 34, 35, 36, 37
WIDE = 256
GROUP = 16
PIECE = 16
VMEM = pl.BlockSpec(memory_space=pltpu.VMEM)
SMEM = pl.BlockSpec(memory_space=pltpu.SMEM)


def params():
    return pltpu.CompilerParams(vmem_limit_bytes=56 * 1024 * 1024)


def unit_rows(raw):
    length = jnp.sqrt(jnp.sum(raw * raw, axis=-1, keepdims=True) + 1e-06)
    return (raw / length, length)


def unit_back(grad, unit, length):
    return (grad - unit * jnp.sum(unit * grad, axis=-1, keepdims=True)) / length


def iota(shape, dim):
    return lax.broadcasted_iota(jnp.int32, shape, dim)


def request_kernel(reps, passes, query_ref, proj_ref, neg_ref, pos_ref, teacher_ref, send_ref, field_ref):
    owners, rows, _ = send_ref.shape
    queries, neg = neg_ref.shape
    query_len = pos_ref.shape[2]
    unit, _ = unit_rows(jnp.dot(query_ref[...], proj_ref[...], preferred_element_type=F32))
    emb = unit.astype(BF16)
    send_ref[:, : emb.shape[0], :] = jnp.broadcast_to(emb[None], (owners,) + emb.shape)
    target = jnp.exp(teacher_ref[...])
    target = target / jnp.sum(target, axis=-1, keepdims=True)
    high = target.astype(BF16).astype(F32)
    rest = target - high
    mid = rest.astype(BF16).astype(F32)
    low = (rest - mid).astype(BF16).astype(F32)
    ids = neg_ref[...]
    owner = lax.div(ids, jnp.int32(reps * passes))
    within = lax.rem(ids, jnp.int32(passes))
    before = (iota((neg, neg), 0) < iota((neg, neg), 1)).astype(F32).astype(BF16)
    total = jnp.zeros((owners, 1), F32)
    meta = jnp.zeros((owners * SLOTS, neg), F32)
    for q in range(queries):
        own = jnp.where(iota((owners, neg), 0) == owner[q : q + 1, :], 1.0, 0.0)
        rank = jnp.dot(own.astype(BF16), before, preferred_element_type=F32) + total
        total = total + jnp.sum(own, axis=1, keepdims=True)
        rank = jnp.sum(own * rank, axis=0, keepdims=True).astype(jnp.int32)
        slot = owner[q : q + 1, :] * SLOTS + rank
        table = jnp.where(iota((owners * SLOTS, neg), 0) == slot, 1.0, 0.0).astype(BF16)
        lines = {
            CODE: (within[q : q + 1, :] * queries + q).astype(F32),
            WHICH: jnp.full((1, neg), float(q), F32),
            VALID: jnp.ones((1, neg), F32),
            HIGH: high[q : q + 1, :],
            MID: mid[q : q + 1, :],
            LOW: low[q : q + 1, :],
        }
        line = iota((neg, neg), 0)
        fields = jnp.zeros((neg, neg), F32)
        for at, value in lines.items():
            fields = fields + jnp.where(line == at, value, 0.0)
        field_ref[...] = fields.T
        field_ref[:, :query_len] = pos_ref[q].astype(F32)
        meta = meta + jnp.dot(table, field_ref[...].astype(BF16), preferred_element_type=F32)
    meta = meta.reshape(owners, SLOTS, neg)
    meta = jnp.concatenate([meta, jnp.zeros((owners, META_ROWS - SLOTS, neg), F32)], axis=1)
    send_ref[:, emb.shape[0] :, :] = meta.astype(BF16)


def embed_kernel(hidden_ref, proj_ref, emb_ref, wide_ref):
    passes, pass_len, _ = hidden_ref.shape
    wide_ref[...] = jnp.zeros_like(wide_ref)
    for p in range(passes):
        unit, _ = unit_rows(jnp.dot(hidden_ref[p], proj_ref[...], preferred_element_type=F32))
        wide_ref[:pass_len, :] = unit
        emb_ref[p] = wide_ref[...].astype(BF16)


def picked_at(meta, group):
    own = meta[group * GROUP : (group + 1) * GROUP]
    return own.reshape(GROUP * SLOTS, own.shape[2]).T


def score_kernel(capacity, block, recv_ref, emb_ref, code_ref, exp_ref, part_ref, table_ref, acc_ref):
    owners = recv_ref.shape[0]
    passes = emb_ref.shape[0]
    queries, query_len = block
    rows = queries * query_len
    emb_dim = recv_ref.shape[2]
    meta = recv_ref[:, rows:, :].astype(F32)[:, :SLOTS, :]
    lane = iota((query_len, WIDE), 1).astype(F32)
    acc_ref[...] = jnp.zeros_like(acc_ref)
    for group in range(owners // GROUP):
        left = recv_ref[group * GROUP : (group + 1) * GROUP, :rows, :].reshape(GROUP * rows, emb_dim)
        for p in range(passes):
            table_ref[p] = lax.dot_general(
                left, emb_ref[p], (((1,), (1,)), ((), ())), preferred_element_type=F32
            )
        spots = picked_at(meta, group)[:query_len]
        for d in range(GROUP):
            for k in range(capacity):
                at = d * SLOTS + k
                code = code_ref[group * GROUP + d, k]
                p = lax.div(code, jnp.int32(queries))
                j = lax.rem(code, jnp.int32(queries))
                start = pl.multiple_of(d * rows + j * query_len, query_len)
                values = table_ref[p, pl.ds(start, query_len), :]
                chosen = jnp.where(spots[:, at : at + 1] == lane, values, 0.0)
                chosen = chosen[:, :emb_dim] + chosen[:, emb_dim:]
                acc_ref[group * GROUP + d, k : k + 1, :] = jnp.sum(chosen, axis=0, keepdims=True)
    scores = jnp.sum(acc_ref[...], axis=-1, keepdims=True)
    exps = jnp.exp(scores) * meta[:, :, VALID : VALID + 1]
    exp_ref[...] = jnp.broadcast_to(exps, exp_ref.shape)
    which = meta[:, :, WHICH : WHICH + 1]
    shape = (owners, 1, emb_dim)
    place = iota(shape, 2) - queries * iota(shape, 0)
    total = jnp.zeros(shape, F32)
    for q in range(queries):
        share = jnp.sum(jnp.where(which == float(q), exps, 0.0), axis=1, keepdims=True)
        total = total + jnp.where(place == q, share, 0.0)
    part_ref[...] = jnp.broadcast_to(jnp.sum(total, axis=0, keepdims=True), part_ref.shape)


def slot_weights(queries, neg, meta, exps, parts):
    owners = exps.shape[0]
    shape = (owners, 1, parts.shape[2])
    place = iota(shape, 2) - queries * iota(shape, 0)
    sums = jnp.sum(parts, axis=0, keepdims=True)
    which = meta[:, :, WHICH : WHICH + 1]
    share = jnp.zeros_like(exps)
    for q in range(queries):
        norm = jnp.sum(jnp.where(place == q, sums, 0.0), axis=-1, keepdims=True)
        share = share + jnp.where(which == float(q), exps / norm, 0.0)
    target = meta[:, :, HIGH : HIGH + 1] + meta[:, :, MID : MID + 1]
    target = target + meta[:, :, LOW : LOW + 1]
    return neg * (share - target) * meta[:, :, VALID : VALID + 1]


def fill_table(capacity, queries, query_len, group, spots, code_ref, weight_ref, table_ref):
    rows = queries * query_len
    lane = iota((query_len, WIDE), 1).astype(F32)
    table_ref[...] = jnp.zeros_like(table_ref)
    for d in range(GROUP):
        for k in range(capacity):
            at = d * SLOTS + k
            code = code_ref[group * GROUP + d, k]
            p = lax.div(code, jnp.int32(queries))
            j = lax.rem(code, jnp.int32(queries))
            start = pl.multiple_of(d * rows + j * query_len, query_len)
            weight = weight_ref[group * GROUP + d, k : k + 1, :]
            weight = jnp.concatenate([weight] * (WIDE // weight.shape[1]), axis=1)
            mask = spots[:, at : at + 1] == lane
            added = jnp.where(mask, weight, 0.0).astype(table_ref.dtype)
            table_ref[p, pl.ds(start, query_len), :] = (
                table_ref[p, pl.ds(start, query_len), :] + added
            )


def query_part_kernel(
    capacity, block, neg, recv_ref, emb_ref, code_ref, exp_ref, part_ref, out_ref, weight_ref, table_ref
):
    owners = recv_ref.shape[0]
    passes = emb_ref.shape[0]
    queries, query_len = block
    rows = queries * query_len
    meta = recv_ref[:, rows:, :].astype(F32)[:, :SLOTS, :]
    weight_ref[...] = slot_weights(queries, neg, meta, exp_ref[...], part_ref[...])
    for group in range(owners // GROUP):
        spots = picked_at(meta, group)[:query_len]
        fill_table(capacity, queries, query_len, group, spots, code_ref, weight_ref, table_ref)
        grad = jnp.zeros((GROUP * rows, emb_ref.shape[2]), F32)
        for p in range(passes):
            grad = grad + jnp.dot(table_ref[p], emb_ref[p], preferred_element_type=F32)
        grad = grad.astype(BF16).reshape(GROUP, rows, emb_ref.shape[2])
        out_ref[group * GROUP : (group + 1) * GROUP] = grad


def passage_kernel(
    capacity,
    block,
    neg,
    recv_ref,
    hidden_ref,
    proj_ref,
    code_ref,
    exp_ref,
    part_ref,
    grad_ref,
    term_ref,
    weight_ref,
    table_ref,
    total_ref,
):
    owners = recv_ref.shape[0]
    passes, pass_len, _ = hidden_ref.shape
    queries, query_len = block
    rows = queries * query_len
    emb_dim = recv_ref.shape[2]
    meta = recv_ref[:, rows:, :].astype(F32)[:, :SLOTS, :]
    weight_ref[...] = slot_weights(queries, neg, meta, exp_ref[...], part_ref[...])
    for group in range(owners // GROUP):
        spots = picked_at(meta, group)[:query_len]
        fill_table(capacity, queries, query_len, group, spots, code_ref, weight_ref, table_ref)
        left = recv_ref[group * GROUP : (group + 1) * GROUP, :rows, :].reshape(GROUP * rows, emb_dim)
        left = left.T
        for p in range(passes):
            grad = jnp.dot(left, table_ref[p], preferred_element_type=F32)
            if group == 0:
                total_ref[p] = grad
            else:
                total_ref[p] = total_ref[p] + grad
    term = jnp.zeros(term_ref.shape, F32)
    for p in range(passes):
        unit, length = unit_rows(jnp.dot(hidden_ref[p], proj_ref[...], preferred_element_type=F32))
        grad = total_ref[p].T[:pass_len]
        raw_grad = unit_back(grad, unit, length).astype(BF16)
        grad_ref[p] = raw_grad
        term = term + lax.dot_general(
            raw_grad, hidden_ref[p], (((0,), (0,)), ((), ())), preferred_element_type=F32
        )
    term_ref[...] = term


def query_kernel(parts_ref, query_ref, proj_ref, term_ref, out_ref):
    hidden = query_ref[...]
    unit, length = unit_rows(jnp.dot(hidden, proj_ref[...], preferred_element_type=F32))
    grad = jnp.sum(parts_ref[...].astype(F32), axis=0)
    raw_grad = unit_back(grad, unit, length).astype(BF16)
    term = term_ref[...] + lax.dot_general(
        raw_grad, hidden, (((0,), (0,)), ((), ())), preferred_element_type=F32
    )
    used = term.shape[1] // PIECE
    out_ref[:used] = term.T.astype(BF16).reshape(used, PIECE, term.shape[0])
    out_ref[used:] = jnp.zeros((out_ref.shape[0] - used,) + out_ref.shape[1:], BF16)


def swap(array, axis):
    return lax.all_to_all(array, axis, split_axis=0, concat_axis=0, tiled=True)


def per_device(query_hidden, passage_hidden, projection, negatives, positions, teacher):
    query_count, query_len, hidden_dim = query_hidden.shape
    pass_count, pass_len, _ = passage_hidden.shape
    emb_dim = projection.shape[1]
    neg_count = negatives.shape[1]
    owners = lax.axis_size("dp")
    reps = lax.axis_size("rep")
    pair_count = query_count * neg_count
    capacity = (pair_count + owners - 2) // (owners - 1)
    rows = query_count * query_len
    block = (query_count, query_len)
    query_flat = query_hidden.reshape(rows, hidden_dim)

    def call(kernel, outs, scratch, specs, *args):
        return pl.pallas_call(
            kernel,
            out_shape=outs,
            in_specs=specs,
            out_specs=jax.tree.map(lambda _: VMEM, outs),
            scratch_shapes=scratch,
            compiler_params=params(),
        )(*args)

    send = call(
        lambda *refs: request_kernel(reps, pass_count, *refs),
        jax.ShapeDtypeStruct((owners, rows + META_ROWS, emb_dim), BF16),
        [pltpu.VMEM((neg_count, neg_count), F32)],
        [VMEM] * 5,
        query_flat,
        projection,
        negatives,
        positions,
        teacher,
    )
    recv = swap(send, "dp")
    emb = call(
        embed_kernel,
        jax.ShapeDtypeStruct((pass_count, WIDE, emb_dim), BF16),
        [pltpu.VMEM((WIDE, emb_dim), F32)],
        [VMEM] * 2,
        passage_hidden,
        projection,
    )
    codes = recv[:, rows : rows + SLOTS, CODE].astype(jnp.int32)
    slot_shape = (owners, SLOTS, emb_dim)
    exps, parts = call(
        lambda *refs: score_kernel(capacity, block, *refs),
        (
            jax.ShapeDtypeStruct(slot_shape, F32),
            jax.ShapeDtypeStruct((owners, 1, emb_dim), F32),
        ),
        [pltpu.VMEM((pass_count, GROUP * rows, WIDE), F32), pltpu.VMEM(slot_shape, F32)],
        [VMEM, VMEM, SMEM],
        recv,
        emb,
        codes,
    )
    parts = swap(parts, "dp")
    table = pltpu.VMEM((pass_count, GROUP * rows, WIDE), BF16)
    query_parts = call(
        lambda *refs: query_part_kernel(capacity, block, neg_count, *refs),
        jax.ShapeDtypeStruct((owners, rows, emb_dim), BF16),
        [pltpu.VMEM(slot_shape, F32), table],
        [VMEM, VMEM, SMEM, VMEM, VMEM],
        recv,
        emb,
        codes,
        exps,
        parts,
    )
    query_parts = swap(query_parts, "dp")
    grad_passages, term = call(
        lambda *refs: passage_kernel(capacity, block, neg_count, *refs),
        (
            jax.ShapeDtypeStruct((pass_count, pass_len, emb_dim), BF16),
            jax.ShapeDtypeStruct((emb_dim, hidden_dim), F32),
        ),
        [pltpu.VMEM(slot_shape, F32), table, pltpu.VMEM((pass_count, emb_dim, WIDE), F32)],
        [VMEM, VMEM, VMEM, SMEM, VMEM, VMEM],
        recv,
        passage_hidden,
        projection,
        codes,
        exps,
        parts,
    )
    pieces = call(
        query_kernel,
        jax.ShapeDtypeStruct((owners, PIECE, emb_dim), BF16),
        [],
        [VMEM] * 4,
        query_parts,
        query_flat,
        projection,
        term,
    )
    pieces = swap(pieces, "dp")
    mine = jnp.sum(pieces.astype(F32), axis=0)
    copies = swap(jnp.broadcast_to(mine[None], (reps,) + mine.shape), "rep")
    scale = 1.0 / math.sqrt(owners * reps * (query_count * query_len + pass_count * pass_len))
    mine = (jnp.sum(copies, axis=0) * scale).astype(BF16)
    copies = swap(jnp.broadcast_to(mine[None], (owners,) + mine.shape), "dp")
    total = copies.reshape(owners * PIECE, emb_dim)[:hidden_dim].astype(F32)
    return (grad_passages, total)


def solution(mesh):
    in_specs = (
        P(("dp", "rep"), None, None),
        P(("dp", "rep"), None, None),
        P(),
        P(("dp", "rep"), None),
        P(("dp", "rep"), None, None),
        P(("dp", "rep"), None),
    )
    out_specs = (P(("dp", "rep"), None, None), P())
    return jax.shard_map(
        per_device, mesh=mesh, in_specs=in_specs, out_specs=out_specs, check_vma=False
    )
```

```python
import math

import jax
import jax.numpy as jnp
from jax import lax
from jax.experimental import pallas as pl
from jax.experimental.pallas import tpu as pltpu
from jax.sharding import Mesh, PartitionSpec as P

F32 = jnp.float32
BF16 = jnp.bfloat16
CORES = 2
CHIPS_X = 4
SLOTS = 8
META_ROWS = CORES * SLOTS
CODE, WHICH, VALID, HIGH, MID, LOW = 32, 33, 34, 35, 36, 37
WIDE = 256
GROUP = 16
VMEM = pl.BlockSpec(memory_space=pltpu.VMEM)
SMEM = pl.BlockSpec(memory_space=pltpu.SMEM)


def params():
    return pltpu.CompilerParams(vmem_limit_bytes=56 * 1024 * 1024)


def unit_rows(raw):
    length = jnp.sqrt(jnp.sum(raw * raw, axis=-1, keepdims=True) + 1e-06)
    return (raw / length, length)


def unit_back(grad, unit, length):
    return (grad - unit * jnp.sum(unit * grad, axis=-1, keepdims=True)) / length


def iota(shape, dim):
    return lax.broadcasted_iota(jnp.int32, shape, dim)


def request_kernel(reps, passes, query_ref, proj_ref, neg_ref, pos_ref, teacher_ref, send_ref):
    chips, _, emb_dim = send_ref.shape
    owners = chips * CORES
    queries, neg = neg_ref.shape
    query_len = pos_ref.shape[1]
    unit, _ = unit_rows(jnp.dot(query_ref[...], proj_ref[...], preferred_element_type=F32))
    emb = unit.astype(BF16)
    send_ref[:, : emb.shape[0], :] = jnp.broadcast_to(emb[None], (chips,) + emb.shape)
    target = jnp.exp(teacher_ref[...])
    target = target / jnp.sum(target, axis=-1, keepdims=True)
    high = target.astype(BF16).astype(F32)
    rest = target - high
    mid = rest.astype(BF16).astype(F32)
    low = (rest - mid).astype(BF16).astype(F32)
    ids = neg_ref[...]
    owner = lax.div(ids, jnp.int32(reps * passes))
    within = lax.rem(ids, jnp.int32(passes))
    before = (iota((neg, neg), 0) < iota((neg, neg), 1)).astype(F32).astype(BF16)
    line = iota((emb_dim - query_len, neg), 0) + query_len
    total = jnp.zeros((owners, 1), F32)
    meta = jnp.zeros((owners * SLOTS, emb_dim), F32)
    for q in range(queries):
        own = jnp.where(iota((owners, neg), 0) == owner[q : q + 1, :], 1.0, 0.0)
        rank = jnp.dot(own.astype(BF16), before, preferred_element_type=F32) + total
        total = total + jnp.sum(own, axis=1, keepdims=True)
        rank = jnp.sum(own * rank, axis=0, keepdims=True).astype(jnp.int32)
        slot = owner[q : q + 1, :] * SLOTS + rank
        table = jnp.where(iota((owners * SLOTS, neg), 0) == slot, 1.0, 0.0).astype(BF16)
        values = {
            CODE: (within[q : q + 1, :] * queries + q).astype(F32),
            WHICH: float(q),
            VALID: 1.0,
            HIGH: high[q : q + 1, :],
            MID: mid[q : q + 1, :],
            LOW: low[q : q + 1, :],
        }
        fields = jnp.zeros(line.shape, F32)
        for at, value in values.items():
            fields = jnp.where(line == at, value, fields)
        fields = jnp.concatenate([pos_ref[q].astype(F32), fields], axis=0)
        meta = meta + jnp.dot(table, fields.T.astype(BF16), preferred_element_type=F32)
    send_ref[:, emb.shape[0] :, :] = meta.reshape(chips, META_ROWS, emb_dim).astype(BF16)


def embed_kernel(hidden_ref, proj_ref, emb_ref, wide_ref):
    passes, pass_len, _ = hidden_ref.shape
    wide_ref[...] = jnp.zeros_like(wide_ref)
    for p in range(passes):
        unit, _ = unit_rows(jnp.dot(hidden_ref[p], proj_ref[...], preferred_element_type=F32))
        wide_ref[:pass_len, :] = unit
        emb_ref[p] = wide_ref[...].astype(BF16)


def picked(meta_ref, group, query_len):
    own = meta_ref[pl.ds(group * GROUP, GROUP)]
    return own.reshape(GROUP * SLOTS, own.shape[2]).T[:query_len]


def slot_code(code_ref, core, d, k, queries):
    code = code_ref[d, core * SLOTS + k]
    return lax.div(code, jnp.int32(queries)), lax.rem(code, jnp.int32(queries))


def places(core, other, shape, queries):
    source = (1 - core) if other else core
    return iota(shape, 2) - queries * (source * shape[0] + iota(shape, 0))


def token_kernel(capacity, block, other, core_ref, code_ref, recv_ref, emb_ref, *refs):
    if other:
        so_far_ref, *refs = refs
    meta_ref, token_ref, exp_ref, part_ref, acc_ref = refs
    chips, _, emb_dim = recv_ref.shape
    queries, query_len = block
    rows = queries * query_len
    core = core_ref[0]
    both = recv_ref[:, rows:, :].astype(F32)
    meta_ref[...] = jnp.where(core == 0, both[:, :SLOTS, :], both[:, SLOTS:, :])
    acc_ref[...] = jnp.zeros_like(acc_ref)
    lane = iota((query_len, WIDE), 1).astype(F32)

    def one_group(group, carry):
        spots = picked(meta_ref, group, query_len)
        for step in range(GROUP):
            d = group * GROUP + step
            for k in range(capacity):
                p, j = slot_code(code_ref, core, d, k, queries)
                at = step * SLOTS + k
                mask = jnp.where(spots[:, at : at + 1] == lane, 1.0, 0.0).astype(BF16)
                token = jnp.dot(mask, emb_ref[p], preferred_element_type=F32)
                token_ref[d, k] = token.astype(BF16)
                start = pl.multiple_of(j * query_len, query_len)
                query = recv_ref[d, pl.ds(start, query_len), :].astype(F32)
                acc_ref[d, k : k + 1, :] = jnp.sum(token * query, axis=0, keepdims=True)
        return carry

    lax.fori_loop(0, chips // GROUP, one_group, 0)
    meta = meta_ref[...]
    exps = jnp.exp(jnp.sum(acc_ref[...], axis=-1, keepdims=True)) * meta[:, :, VALID : VALID + 1]
    exp_ref[...] = jnp.broadcast_to(exps, exp_ref.shape)
    which = meta[:, :, WHICH : WHICH + 1]
    place = places(core, other, (chips, 1, emb_dim), queries)
    total = jnp.zeros(place.shape, F32)
    for q in range(queries):
        share = jnp.sum(jnp.where(which == float(q), exps, 0.0), axis=1, keepdims=True)
        total = total + jnp.where(place == q, share, 0.0)
    total = jnp.sum(total, axis=0, keepdims=True)
    if other:
        total = total + so_far_ref[...]
    part_ref[...] = jnp.broadcast_to(total, part_ref.shape)


def weight_kernel(capacity, block, neg, other, core_ref, parts_ref, meta_ref, exp_ref, token_ref, out_ref, weight_ref):
    queries, query_len = block
    chips, _, emb_dim = exp_ref.shape
    meta = meta_ref[...]
    exps = exp_ref[...]
    place = places(core_ref[0], other, (chips, 1, emb_dim), queries)
    sums = jnp.sum(parts_ref[...], axis=0, keepdims=True)
    which = meta[:, :, WHICH : WHICH + 1]
    share = jnp.zeros_like(exps)
    for q in range(queries):
        norm = jnp.sum(jnp.where(place == q, sums, 0.0), axis=-1, keepdims=True)
        share = share + jnp.where(which == float(q), exps / norm, 0.0)
    target = meta[:, :, HIGH : HIGH + 1] + meta[:, :, MID : MID + 1]
    target = target + meta[:, :, LOW : LOW + 1]
    weight_ref[...] = neg * (share - target) * meta[:, :, VALID : VALID + 1]

    def one_device(d, carry):
        chosen = meta_ref[d][:, WHICH : WHICH + 1]
        weights = weight_ref[d]
        for q in range(queries):
            scale = jnp.where(chosen == float(q), weights, 0.0)
            grad = jnp.zeros((query_len, emb_dim), F32)
            for k in range(capacity):
                grad = grad + scale[k : k + 1, :] * token_ref[d, k].astype(F32)
            out_ref[d, q * query_len : (q + 1) * query_len, :] = grad.astype(BF16)
        return carry

    lax.fori_loop(0, chips, one_device, 0, unroll=4)


def passage_kernel(capacity, block, core_ref, hidden_ref, proj_ref, *refs):
    halves = [refs[4 * h : 4 * h + 4] for h in range(CORES)]
    grad_ref, term_ref, table_ref, total_ref = refs[4 * CORES :]
    passes, pass_len, _ = hidden_ref.shape
    queries, query_len = block
    rows = queries * query_len
    core = core_ref[0]
    lane = iota((query_len, WIDE), 1).astype(F32)
    total_ref[...] = jnp.zeros_like(total_ref)
    for code_ref, recv_ref, meta_ref, weight_ref in halves:
        chips, _, emb_dim = recv_ref.shape

        def one_group(group, carry):
            spots = picked(meta_ref, group, query_len)
            table_ref[...] = jnp.zeros_like(table_ref)
            for step in range(GROUP):
                d = group * GROUP + step
                for k in range(capacity):
                    p, j = slot_code(code_ref, core, d, k, queries)
                    at = step * SLOTS + k
                    start = pl.multiple_of(step * rows + j * query_len, query_len)
                    weight = weight_ref[d, k : k + 1, :]
                    weight = jnp.concatenate([weight] * (WIDE // emb_dim), axis=1)
                    added = jnp.where(spots[:, at : at + 1] == lane, weight, 0.0).astype(BF16)
                    table_ref[p, pl.ds(start, query_len), :] = (
                        table_ref[p, pl.ds(start, query_len), :] + added
                    )
            left = recv_ref[pl.ds(group * GROUP, GROUP), :rows, :].reshape(GROUP * rows, emb_dim)
            left = left.T
            for p in range(passes):
                total_ref[p] = total_ref[p] + jnp.dot(
                    left, table_ref[p], preferred_element_type=F32
                )
            return carry

        lax.fori_loop(0, chips // GROUP, one_group, 0)
    term = jnp.zeros(term_ref.shape, F32)
    for p in range(passes):
        unit, length = unit_rows(jnp.dot(hidden_ref[p], proj_ref[...], preferred_element_type=F32))
        grad = total_ref[p].T[:pass_len]
        raw_grad = unit_back(grad, unit, length).astype(BF16)
        grad_ref[p] = raw_grad
        term = term + lax.dot_general(
            raw_grad, hidden_ref[p], (((0,), (0,)), ((), ())), preferred_element_type=F32
        )
    term_ref[...] = term


def query_kernel(parts_ref, query_ref, proj_ref, term_ref, out_ref):
    hidden = query_ref[...]
    unit, length = unit_rows(jnp.dot(hidden, proj_ref[...], preferred_element_type=F32))
    grad = jnp.sum(parts_ref[...].astype(F32), axis=0)
    raw_grad = unit_back(grad, unit, length).astype(BF16)
    term = term_ref[...] + lax.dot_general(
        raw_grad, hidden, (((0,), (0,)), ((), ())), preferred_element_type=F32
    )
    out_ref[...] = term.T.reshape(out_ref.shape).astype(BF16)


def swap(array, axes):
    return lax.all_to_all(array, axes, split_axis=0, concat_axis=0, tiled=True)


def to_other_core(array):
    return lax.ppermute(array, "core", [(c, CORES - 1 - c) for c in range(CORES)])


def per_device(query_hidden, passage_hidden, projection, negatives, positions, teacher):
    query_count, query_len, hidden_dim = query_hidden.shape
    pass_count, pass_len, _ = passage_hidden.shape
    emb_dim = projection.shape[1]
    neg_count = negatives.shape[1]
    chips = lax.axis_size("x") * lax.axis_size("z")
    owners = chips * CORES
    reps = lax.axis_size("rep")
    pair_count = query_count * neg_count
    capacity = (pair_count + owners - 2) // (owners - 1)
    rows = query_count * query_len
    block = (query_count, query_len)
    query_flat = query_hidden.reshape(rows, hidden_dim)
    core = lax.axis_index("core").reshape(1)

    def call(kernel, outs, scratch, scalars, *args):
        return pl.pallas_call(
            kernel,
            out_shape=outs,
            in_specs=[SMEM if n in scalars else VMEM for n in range(len(args))],
            out_specs=jax.tree.map(lambda _: VMEM, outs),
            scratch_shapes=scratch,
            compiler_params=params(),
        )(*args)

    shape = jax.ShapeDtypeStruct
    send = call(
        lambda *refs: request_kernel(reps, pass_count, *refs),
        shape((chips, rows + META_ROWS, emb_dim), BF16),
        [],
        (),
        query_flat,
        projection,
        negatives,
        jnp.swapaxes(positions, 1, 2),
        teacher,
    )
    near = swap(send, ("x", "z"))
    far = to_other_core(near)
    emb = call(
        embed_kernel,
        shape((pass_count, WIDE, emb_dim), BF16),
        [pltpu.VMEM((WIDE, emb_dim), F32)],
        (),
        passage_hidden,
        projection,
    )
    slot_shape = (chips, SLOTS, emb_dim)
    halves = []
    so_far = []
    for other, recv in ((False, near), (True, far)):
        codes = recv[:, rows:, CODE].astype(jnp.int32)
        meta, tokens, exps, part = call(
            lambda *refs: token_kernel(capacity, block, other, *refs),
            (
                shape(slot_shape, F32),
                shape((chips, capacity, query_len, emb_dim), BF16),
                shape(slot_shape, F32),
                shape((owners if other else 1, 1, emb_dim), F32),
            ),
            [pltpu.VMEM(slot_shape, F32)],
            (0, 1),
            core,
            codes,
            recv,
            emb,
            *so_far,
        )
        so_far = [part]
        halves.append((codes, recv, meta, exps, tokens))
    parts = swap(part, ("x", "z", "core"))

    def weigh(other):
        codes, recv, meta, exps, tokens = halves[other]
        return call(
            lambda *refs: weight_kernel(capacity, block, neg_count, other, *refs),
            (shape((chips, rows, emb_dim), BF16), shape(slot_shape, F32)),
            [],
            (0,),
            core,
            parts,
            meta,
            exps,
            tokens,
        )

    far_part, far_weight = weigh(True)
    far_part = to_other_core(far_part)
    near_part, near_weight = weigh(False)
    query_parts = (near_part.astype(F32) + far_part.astype(F32)).astype(BF16)
    query_parts, near_weight = lax.optimization_barrier((query_parts, near_weight))
    query_parts = swap(query_parts, ("x", "z"))
    passage_args = []
    for (codes, recv, meta, _, _), weight in zip(halves, (near_weight, far_weight)):
        passage_args += [codes, recv, meta, weight]
    grad_passages, term = call(
        lambda *refs: passage_kernel(capacity, block, *refs),
        (
            shape((pass_count, pass_len, emb_dim), BF16),
            shape((emb_dim, hidden_dim), F32),
        ),
        [
            pltpu.VMEM((pass_count, GROUP * rows, WIDE), BF16),
            pltpu.VMEM((pass_count, emb_dim, WIDE), F32),
        ],
        (0, 3, 7),
        core,
        passage_hidden,
        projection,
        *passage_args,
    )
    groups = lax.axis_size(("x", "core", "rep"))
    pieces = call(
        query_kernel,
        shape((groups, hidden_dim // groups, emb_dim), BF16),
        [],
        (),
        query_parts,
        query_flat,
        projection,
        term,
    )
    pieces = swap(pieces, ("x", "core", "rep"))
    mine = jnp.sum(pieces.astype(F32), axis=0).astype(BF16)
    copies = swap(jnp.broadcast_to(mine[None], (lax.axis_size("z"),) + mine.shape), "z")
    scale = 1.0 / math.sqrt(owners * reps * (query_count * query_len + pass_count * pass_len))
    mine = (jnp.sum(copies.astype(F32), axis=0) * scale).astype(BF16)
    copies = swap(jnp.broadcast_to(mine[None], (groups,) + mine.shape), ("x", "core", "rep"))
    return (grad_passages, copies.reshape(hidden_dim, emb_dim).astype(F32))


def solution(mesh):
    devices = mesh.devices.reshape(CHIPS_X, -1, CORES, mesh.shape["rep"])
    mesh = Mesh(devices, ("x", "z", "core", "rep"))
    whole = ("x", "z", "core", "rep")
    in_specs = (
        P(whole, None, None),
        P(whole, None, None),
        P(),
        P(whole, None),
        P(whole, None, None),
        P(whole, None),
    )
    out_specs = (P(whole, None, None), P())
    return jax.shard_map(
        per_device, mesh=mesh, in_specs=in_specs, out_specs=out_specs, check_vma=False
    )
```

```python
import math

import jax
import jax.numpy as jnp
from jax import lax
from jax.experimental import pallas as pl
from jax.experimental.pallas import tpu as pltpu
from jax.sharding import Mesh, PartitionSpec as P

F32 = jnp.float32
BF16 = jnp.bfloat16
CORES = 2
CHIPS_X = 4
SLOTS = 8
META_ROWS = 8
PER_CORE = 2
CODE, WHICH, VALID, HIGH, MID, LOW = range(6)
WIDE = 256
GROUP = 16
VMEM = pl.BlockSpec(memory_space=pltpu.VMEM)
SMEM = pl.BlockSpec(memory_space=pltpu.SMEM)


def params():
    return pltpu.CompilerParams(vmem_limit_bytes=56 * 1024 * 1024)


def unit_rows(raw):
    length = jnp.sqrt(jnp.sum(raw * raw, axis=-1, keepdims=True) + 1e-06)
    return (raw / length, length)


def unit_back(grad, unit, length):
    return (grad - unit * jnp.sum(unit * grad, axis=-1, keepdims=True)) / length


def iota(shape, dim):
    return lax.broadcasted_iota(jnp.int32, shape, dim)


def request_kernel(reps, passes, query_ref, proj_ref, neg_ref, pos_ref, teacher_ref, send_ref, meta_ref):
    chips, _, emb_dim = send_ref.shape
    owners = chips * CORES
    queries, neg = neg_ref.shape
    query_len = pos_ref.shape[1]
    per_row = emb_dim // query_len
    unit, _ = unit_rows(jnp.dot(query_ref[...], proj_ref[...], preferred_element_type=F32))
    emb = unit.astype(BF16)
    send_ref[:, : emb.shape[0], :] = jnp.broadcast_to(emb[None], (chips,) + emb.shape)
    target = jnp.exp(teacher_ref[...])
    target = target / jnp.sum(target, axis=-1, keepdims=True)
    high = target.astype(BF16).astype(F32)
    rest = target - high
    mid = rest.astype(BF16).astype(F32)
    low = (rest - mid).astype(BF16).astype(F32)
    ids = neg_ref[...]
    owner = lax.div(ids, jnp.int32(reps * passes))
    within = lax.rem(ids, jnp.int32(passes))
    before = (iota((neg, neg), 0) < iota((neg, neg), 1)).astype(F32).astype(BF16)
    total = jnp.zeros((owners, 1), F32)
    meta = [jnp.zeros((chips, PER_CORE * emb_dim), F32) for _ in range(CORES)]
    for q in range(queries):
        mine = owner[q : q + 1, :]
        own = jnp.where(iota((owners, neg), 0) == mine, 1.0, 0.0)
        rank = jnp.dot(own.astype(BF16), before, preferred_element_type=F32) + total
        total = total + jnp.sum(own, axis=1, keepdims=True)
        rank = jnp.sum(own * rank, axis=0, keepdims=True).astype(jnp.int32)
        spots = pos_ref[q].astype(F32)
        lines = [jnp.where(rank == k, spots, 0.0) for k in range(per_row + 1)]
        values = {
            CODE: (within[q : q + 1, :] * queries + q).astype(F32),
            WHICH: jnp.full((1, neg), float(q), F32),
            VALID: jnp.ones((1, neg), F32),
            HIGH: high[q : q + 1, :],
            MID: mid[q : q + 1, :],
            LOW: low[q : q + 1, :],
        }
        line = iota((SLOTS, neg), 0)
        lines += [jnp.where(line == rank, values[at], 0.0) for at in sorted(values)]
        lines = jnp.concatenate(lines, axis=0)
        extra = PER_CORE * emb_dim - lines.shape[0]
        lines = jnp.concatenate([lines, jnp.zeros((extra, neg), F32)], axis=0)
        fields = jnp.concatenate([lines[:emb_dim].T, lines[emb_dim:].T], axis=1).astype(BF16)
        for c in range(CORES):
            to = jnp.where(iota((chips, neg), 0) * CORES + c == mine, 1.0, 0.0).astype(BF16)
            meta[c] = meta[c] + jnp.dot(to, fields, preferred_element_type=F32)
    meta_ref[...] = jnp.zeros_like(meta_ref)
    for c in range(CORES):
        for r in range(PER_CORE):
            meta_ref[:, c * PER_CORE + r, :] = meta[c][:, r * emb_dim : (r + 1) * emb_dim]
    send_ref[:, emb.shape[0] :, :] = meta_ref[...].astype(BF16)


def embed_kernel(hidden_ref, proj_ref, emb_ref, wide_ref):
    passes, pass_len, _ = hidden_ref.shape
    wide_ref[...] = jnp.zeros_like(wide_ref)
    for p in range(passes):
        unit, _ = unit_rows(jnp.dot(hidden_ref[p], proj_ref[...], preferred_element_type=F32))
        wide_ref[:pass_len, :] = unit
        emb_ref[p] = wide_ref[...].astype(BF16)


def field(extra, query_len, name):
    lanes = extra.shape[1]
    return pltpu.roll(extra, lanes - query_len - name * SLOTS, 1)


def picked(spots_ref, extra_ref, group, query_len, capacity):
    spots = spots_ref[pl.ds(pl.multiple_of(group * GROUP, GROUP), GROUP), :].T
    extra = extra_ref[pl.ds(pl.multiple_of(group * GROUP, GROUP), GROUP), :].T
    both = jnp.concatenate([spots, extra[:query_len]], axis=0)
    return [both[k * query_len : (k + 1) * query_len] for k in range(capacity)]


def slot_code(code_ref, d, k, query_len, queries):
    code = code_ref[d, query_len + k]
    return lax.div(code, jnp.int32(queries)), lax.rem(code, jnp.int32(queries))


def places(core, other, shape, queries):
    source = (1 - core) if other else core
    return iota(shape, 1) - queries * (source * shape[0] + iota(shape, 0))


def token_kernel(capacity, block, other, core_ref, recv_ref, emb_ref, *refs):
    if other:
        so_far_ref, *refs = refs
    spots_ref, extra_ref, code_ref, token_ref, exp_ref, part_ref, both_ref, acc_ref, scalar_ref, sem = refs
    chips, _, emb_dim = recv_ref.shape
    queries, query_len = block
    rows = queries * query_len
    core = core_ref[0]
    both_ref[...] = recv_ref[:, rows:, :].astype(F32)
    spots_ref[...] = jnp.where(core == 0, both_ref[:, 0, :], both_ref[:, PER_CORE, :])
    extra = jnp.where(core == 0, both_ref[:, 1, :], both_ref[:, PER_CORE + 1, :])
    extra_ref[...] = extra
    code_ref[...] = extra.astype(jnp.int32)
    copy = pltpu.make_async_copy(code_ref, scalar_ref, sem)
    copy.start()
    acc_ref[...] = jnp.zeros_like(acc_ref)
    copy.wait()
    lane = iota((query_len, WIDE), 1).astype(F32)

    def one_group(group, carry):
        spots = picked(spots_ref, extra_ref, group, query_len, capacity)
        for step in range(GROUP):
            d = group * GROUP + step
            for k in range(capacity):
                p, j = slot_code(scalar_ref, d, k, query_len, queries)
                mask = jnp.where(spots[k][:, step : step + 1] == lane, 1.0, 0.0).astype(BF16)
                token = jnp.dot(mask, emb_ref[p], preferred_element_type=F32)
                token_ref[d, k] = token.astype(BF16)
                start = pl.multiple_of(j * query_len, query_len)
                query = recv_ref[d, pl.ds(start, query_len), :].astype(F32)
                acc_ref[k, pl.ds(d, 1), :] = jnp.sum(token * query, axis=0, keepdims=True)
        return carry

    lax.fori_loop(0, chips // GROUP, one_group, 0)
    shape = (chips, emb_dim)
    at = iota(shape, 1)
    scores = jnp.zeros(shape, F32)
    for k in range(capacity):
        scores = jnp.where(at == k, jnp.sum(acc_ref[k], axis=-1, keepdims=True), scores)
    exps = jnp.where(at < capacity, jnp.exp(scores) * field(extra, query_len, VALID), 0.0)
    exp_ref[...] = exps
    which = field(extra, query_len, WHICH)
    place = places(core, other, shape, queries)
    total = jnp.zeros(shape, F32)
    for q in range(queries):
        share = jnp.sum(jnp.where(which == float(q), exps, 0.0), axis=1, keepdims=True)
        total = jnp.where(place == q, share, total)
    total = jnp.sum(total, axis=0, keepdims=True)
    if other:
        total = total + so_far_ref[0]
    part_ref[...] = jnp.broadcast_to(total[None], part_ref.shape)


def weight_kernel(capacity, block, neg, other, core_ref, parts_ref, extra_ref, exp_ref, token_ref, out_ref, weight_ref, scale_ref):
    queries, query_len = block
    chips, emb_dim = exp_ref.shape
    exps = exp_ref[...]
    extra = extra_ref[...]
    place = places(core_ref[0], other, exps.shape, queries)
    sums = jnp.sum(parts_ref[...], axis=0)
    which = field(extra, query_len, WHICH)
    share = jnp.zeros_like(exps)
    for q in range(queries):
        norm = jnp.sum(jnp.where(place == q, sums, 0.0), axis=-1, keepdims=True)
        share = jnp.where(which == float(q), exps / norm, share)
    target = field(extra, query_len, HIGH) + field(extra, query_len, MID)
    target = target + field(extra, query_len, LOW)
    weights = neg * (share - target) * field(extra, query_len, VALID)
    weights = jnp.where(iota(exps.shape, 1) < capacity, weights, 0.0)
    for k in range(capacity):
        weight_ref[k] = jnp.broadcast_to(weights[:, k : k + 1], exps.shape)
    for q in range(queries):
        scale = jnp.where(which == float(q), weights, 0.0)
        for k in range(capacity):
            scale_ref[q * capacity + k] = jnp.broadcast_to(scale[:, k : k + 1], exps.shape)

    def one_device(d, carry):
        tokens = [token_ref[d, k].astype(F32) for k in range(capacity)]
        for q in range(queries):
            grad = scale_ref[q * capacity, pl.ds(d, 1), :] * tokens[0]
            for k in range(1, capacity):
                grad = grad + scale_ref[q * capacity + k, pl.ds(d, 1), :] * tokens[k]
            out_ref[d, q * query_len : (q + 1) * query_len, :] = grad.astype(BF16)
        return carry

    lax.fori_loop(0, chips, one_device, 0, unroll=8)


def add_kernel(left_ref, right_ref, out_ref):
    out_ref[...] = (left_ref[...].astype(F32) + right_ref[...].astype(F32)).astype(BF16)


def passage_kernel(capacity, block, core_ref, hidden_ref, proj_ref, *refs):
    halves = [refs[5 * h : 5 * h + 5] for h in range(CORES)]
    grad_ref, term_ref, table_ref, total_ref = refs[5 * CORES :]
    passes, pass_len, _ = hidden_ref.shape
    queries, query_len = block
    rows = queries * query_len
    lane = iota((query_len, WIDE), 1).astype(F32)
    total_ref[...] = jnp.zeros_like(total_ref)
    for code_ref, recv_ref, spots_ref, extra_ref, weight_ref in halves:
        chips, _, emb_dim = recv_ref.shape

        def one_group(group, carry):
            spots = picked(spots_ref, extra_ref, group, query_len, capacity)
            table_ref[...] = jnp.zeros_like(table_ref)
            for step in range(GROUP):
                d = group * GROUP + step
                for k in range(capacity):
                    p, j = slot_code(code_ref, d, k, query_len, queries)
                    start = pl.multiple_of(step * rows + j * query_len, query_len)
                    weight = weight_ref[k, pl.ds(d, 1), :]
                    weight = jnp.concatenate([weight] * (WIDE // emb_dim), axis=1)
                    added = jnp.where(spots[k][:, step : step + 1] == lane, weight, 0.0).astype(BF16)
                    table_ref[p, pl.ds(start, query_len), :] = (
                        table_ref[p, pl.ds(start, query_len), :] + added
                    )
            left = recv_ref[pl.ds(group * GROUP, GROUP), :rows, :].reshape(GROUP * rows, emb_dim)
            left = left.T
            for p in range(passes):
                total_ref[p] = total_ref[p] + jnp.dot(
                    left, table_ref[p], preferred_element_type=F32
                )
            return carry

        lax.fori_loop(0, chips // GROUP, one_group, 0)
    term = jnp.zeros(term_ref.shape, F32)
    for p in range(passes):
        unit, length = unit_rows(jnp.dot(hidden_ref[p], proj_ref[...], preferred_element_type=F32))
        grad = total_ref[p].T[:pass_len]
        raw_grad = unit_back(grad, unit, length).astype(BF16)
        grad_ref[p] = raw_grad
        term = term + lax.dot_general(
            raw_grad, hidden_ref[p], (((0,), (0,)), ((), ())), preferred_element_type=F32
        )
    term_ref[...] = term


def query_kernel(parts_ref, query_ref, proj_ref, term_ref, out_ref):
    hidden = query_ref[...]
    unit, length = unit_rows(jnp.dot(hidden, proj_ref[...], preferred_element_type=F32))
    grad = jnp.sum(parts_ref[...].astype(F32), axis=0)
    raw_grad = unit_back(grad, unit, length).astype(BF16)
    term = term_ref[...] + lax.dot_general(
        raw_grad, hidden, (((0,), (0,)), ((), ())), preferred_element_type=F32
    )
    out_ref[...] = term.T.reshape(out_ref.shape).astype(BF16)


def swap(array, axes):
    return lax.all_to_all(array, axes, split_axis=0, concat_axis=0, tiled=True)


def to_other_core(array):
    return lax.ppermute(array, "core", [(c, CORES - 1 - c) for c in range(CORES)])


def per_device(query_hidden, passage_hidden, projection, negatives, positions, teacher):
    query_count, query_len, hidden_dim = query_hidden.shape
    pass_count, pass_len, _ = passage_hidden.shape
    emb_dim = projection.shape[1]
    neg_count = negatives.shape[1]
    chips = lax.axis_size("x") * lax.axis_size("z")
    owners = chips * CORES
    reps = lax.axis_size("rep")
    pair_count = query_count * neg_count
    capacity = (pair_count + owners - 2) // (owners - 1)
    rows = query_count * query_len
    block = (query_count, query_len)
    query_flat = query_hidden.reshape(rows, hidden_dim)
    core = lax.axis_index("core").reshape(1)

    def call(kernel, outs, scratch, scalars, *args):
        return pl.pallas_call(
            kernel,
            out_shape=outs,
            in_specs=[SMEM if n in scalars else VMEM for n in range(len(args))],
            out_specs=jax.tree.map(lambda _: VMEM, outs),
            scratch_shapes=scratch,
            compiler_params=params(),
        )(*args)

    shape = jax.ShapeDtypeStruct
    send = call(
        lambda *refs: request_kernel(reps, pass_count, *refs),
        shape((chips, rows + META_ROWS, emb_dim), BF16),
        [pltpu.VMEM((chips, META_ROWS, emb_dim), F32)],
        (),
        query_flat,
        projection,
        negatives,
        jnp.swapaxes(positions, 1, 2),
        teacher,
    )
    near = swap(send, ("x", "z"))
    emb = call(
        embed_kernel,
        shape((pass_count, WIDE, emb_dim), BF16),
        [pltpu.VMEM((WIDE, emb_dim), F32)],
        (),
        passage_hidden,
        projection,
    )
    near, emb = lax.optimization_barrier((near, emb))
    far = to_other_core(near)
    slot_shape = (chips, emb_dim)
    halves = []
    so_far = []
    for other, recv in ((False, near), (True, far)):
        spots, extra, codes, tokens, exps, part = call(
            lambda *refs: token_kernel(capacity, block, other, *refs),
            (
                shape(slot_shape, F32),
                shape(slot_shape, F32),
                shape(slot_shape, jnp.int32),
                shape((chips, capacity, query_len, emb_dim), BF16),
                shape(slot_shape, F32),
                shape((owners if other else 1, 1, emb_dim), F32),
            ),
            [
                pltpu.VMEM((chips, META_ROWS, emb_dim), F32),
                pltpu.VMEM((capacity,) + slot_shape, F32),
                pltpu.SMEM(slot_shape, jnp.int32),
                pltpu.SemaphoreType.DMA,
            ],
            (0,),
            core,
            recv,
            emb,
            *so_far,
        )
        so_far = [part]
        halves.append((codes, recv, spots, extra, exps, tokens))
    parts = swap(part, ("x", "z", "core"))

    def weigh(other):
        _, _, _, extra, exps, tokens = halves[other]
        return call(
            lambda *refs: weight_kernel(capacity, block, neg_count, other, *refs),
            (shape((chips, rows, emb_dim), BF16), shape((capacity,) + slot_shape, F32)),
            [pltpu.VMEM((query_count * capacity,) + slot_shape, F32)],
            (0,),
            core,
            parts,
            extra,
            exps,
            tokens,
        )

    far_part, far_weight = weigh(True)
    far_part = to_other_core(far_part)
    near_part, near_weight = weigh(False)
    query_parts = call(add_kernel, shape(near_part.shape, BF16), [], (), near_part, far_part)
    query_parts, near_weight = lax.optimization_barrier((query_parts, near_weight))
    query_parts = swap(query_parts, ("x", "z"))
    passage_args = []
    for (codes, recv, spots, extra, _, _), weight in zip(halves, (near_weight, far_weight)):
        passage_args += [codes, recv, spots, extra, weight]
    grad_passages, term = call(
        lambda *refs: passage_kernel(capacity, block, *refs),
        (
            shape((pass_count, pass_len, emb_dim), BF16),
            shape((emb_dim, hidden_dim), F32),
        ),
        [
            pltpu.VMEM((pass_count, GROUP * rows, WIDE), BF16),
            pltpu.VMEM((pass_count, emb_dim, WIDE), F32),
        ],
        (0, 3, 8),
        core,
        passage_hidden,
        projection,
        *passage_args,
    )
    groups = lax.axis_size(("x", "core", "rep"))
    pieces = call(
        query_kernel,
        shape((groups, hidden_dim // groups, emb_dim), BF16),
        [],
        (),
        query_parts,
        query_flat,
        projection,
        term,
    )
    pieces = swap(pieces, ("x", "core", "rep"))
    mine = jnp.sum(pieces.astype(F32), axis=0).astype(BF16)
    copies = swap(jnp.broadcast_to(mine[None], (lax.axis_size("z"),) + mine.shape), "z")
    scale = 1.0 / math.sqrt(owners * reps * (query_count * query_len + pass_count * pass_len))
    mine = (jnp.sum(copies.astype(F32), axis=0) * scale).astype(BF16)
    copies = swap(jnp.broadcast_to(mine[None], (groups,) + mine.shape), ("x", "core", "rep"))
    return (grad_passages, copies.reshape(hidden_dim, emb_dim).astype(F32))


def solution(mesh):
    devices = mesh.devices.reshape(CHIPS_X, -1, CORES, mesh.shape["rep"])
    mesh = Mesh(devices, ("x", "z", "core", "rep"))
    whole = ("x", "z", "core", "rep")
    in_specs = (
        P(whole, None, None),
        P(whole, None, None),
        P(),
        P(whole, None),
        P(whole, None, None),
        P(whole, None),
    )
    out_specs = (P(whole, None, None), P())
    return jax.shard_map(
        per_device, mesh=mesh, in_specs=in_specs, out_specs=out_specs, check_vma=False
    )
```

```python
import math

import jax
import jax.numpy as jnp
from jax import lax
from jax.experimental import pallas as pl
from jax.experimental.pallas import tpu as pltpu
from jax.sharding import Mesh, PartitionSpec as P

F32 = jnp.float32
BF16 = jnp.bfloat16
CORES = 2
CHIPS_X = 4
SLOTS = 8
META_ROWS = 8
PER_CORE = 2
CODE, WHICH, VALID, HIGH, MID, LOW = range(6)
WIDE = 256
GROUP = 16
VMEM = pl.BlockSpec(memory_space=pltpu.VMEM)
SMEM = pl.BlockSpec(memory_space=pltpu.SMEM)


def params(mb):
    return pltpu.CompilerParams(vmem_limit_bytes=mb * 1024 * 1024)


def unit_rows(raw):
    length = jnp.sqrt(jnp.sum(raw * raw, axis=-1, keepdims=True) + 1e-06)
    return (raw / length, length)


def unit_back(grad, unit, length):
    return (grad - unit * jnp.sum(unit * grad, axis=-1, keepdims=True)) / length


def iota(shape, dim):
    return lax.broadcasted_iota(jnp.int32, shape, dim)


def request_kernel(reps, passes, query_ref, proj_ref, neg_ref, pos_ref, teacher_ref, send_ref, meta_ref):
    chips, _, emb_dim = send_ref.shape
    owners = chips * CORES
    queries, neg = neg_ref.shape
    query_len = pos_ref.shape[1]
    per_row = emb_dim // query_len
    unit, _ = unit_rows(jnp.dot(query_ref[...], proj_ref[...], preferred_element_type=F32))
    emb = unit.astype(BF16)
    send_ref[:, : emb.shape[0], :] = jnp.broadcast_to(emb[None], (chips,) + emb.shape)
    target = jnp.exp(teacher_ref[...])
    target = target / jnp.sum(target, axis=-1, keepdims=True)
    high = target.astype(BF16).astype(F32)
    rest = target - high
    mid = rest.astype(BF16).astype(F32)
    low = (rest - mid).astype(BF16).astype(F32)
    ids = neg_ref[...]
    owner = lax.div(ids, jnp.int32(reps * passes))
    within = lax.rem(ids, jnp.int32(passes))
    before = (iota((neg, neg), 0) < iota((neg, neg), 1)).astype(F32).astype(BF16)
    total = jnp.zeros((owners, 1), F32)
    meta = [jnp.zeros((chips, PER_CORE * emb_dim), F32) for _ in range(CORES)]
    for q in range(queries):
        mine = owner[q : q + 1, :]
        own = jnp.where(iota((owners, neg), 0) == mine, 1.0, 0.0)
        rank = jnp.dot(own.astype(BF16), before, preferred_element_type=F32) + total
        total = total + jnp.sum(own, axis=1, keepdims=True)
        rank = jnp.sum(own * rank, axis=0, keepdims=True).astype(jnp.int32)
        spots = pos_ref[q].astype(F32)
        lines = [jnp.where(rank == k, spots, 0.0) for k in range(per_row + 1)]
        values = {
            CODE: (within[q : q + 1, :] * queries + q).astype(F32),
            WHICH: jnp.full((1, neg), float(q), F32),
            VALID: jnp.ones((1, neg), F32),
            HIGH: high[q : q + 1, :],
            MID: mid[q : q + 1, :],
            LOW: low[q : q + 1, :],
        }
        line = iota((SLOTS, neg), 0)
        lines += [jnp.where(line == rank, values[at], 0.0) for at in sorted(values)]
        lines = jnp.concatenate(lines, axis=0)
        extra = PER_CORE * emb_dim - lines.shape[0]
        lines = jnp.concatenate([lines, jnp.zeros((extra, neg), F32)], axis=0)
        fields = jnp.concatenate([lines[:emb_dim].T, lines[emb_dim:].T], axis=1).astype(BF16)
        for c in range(CORES):
            to = jnp.where(iota((chips, neg), 0) * CORES + c == mine, 1.0, 0.0).astype(BF16)
            meta[c] = meta[c] + jnp.dot(to, fields, preferred_element_type=F32)
    meta_ref[...] = jnp.zeros_like(meta_ref)
    for c in range(CORES):
        for r in range(PER_CORE):
            meta_ref[:, c * PER_CORE + r, :] = meta[c][:, r * emb_dim : (r + 1) * emb_dim]
    send_ref[:, emb.shape[0] :, :] = meta_ref[...].astype(BF16)


def embed_kernel(hidden_ref, proj_ref, emb_ref, unit_ref, inverse_ref):
    passes, pass_len, _ = hidden_ref.shape
    unit_ref[...] = jnp.zeros_like(unit_ref)
    for p in range(passes):
        unit, length = unit_rows(jnp.dot(hidden_ref[p], proj_ref[...], preferred_element_type=F32))
        unit_ref[p, :pass_len, :] = unit
        inverse_ref[p, :pass_len, :] = jnp.broadcast_to(1.0 / length, unit.shape)
        emb_ref[p] = unit_ref[p].astype(BF16)


def field(extra, query_len, name):
    lanes = extra.shape[1]
    return pltpu.roll(extra, lanes - query_len - name * SLOTS, 1)


def picked(spots_ref, extra_ref, group, query_len, capacity):
    spots = spots_ref[pl.ds(pl.multiple_of(group * GROUP, GROUP), GROUP), :].T
    extra = extra_ref[pl.ds(pl.multiple_of(group * GROUP, GROUP), GROUP), :].T
    both = jnp.concatenate([spots, extra[:query_len]], axis=0)
    return [both[k * query_len : (k + 1) * query_len] for k in range(capacity)]


def unpack(core, recv_ref, rows, both_ref, spots_ref, extra_ref, code_ref, scalar_ref, sem):
    both_ref[...] = recv_ref[:, rows:, :].astype(F32)
    spots_ref[...] = jnp.where(core == 0, both_ref[:, 0, :], both_ref[:, PER_CORE, :])
    extra = jnp.where(core == 0, both_ref[:, 1, :], both_ref[:, PER_CORE + 1, :])
    extra_ref[...] = extra
    code_ref[...] = extra.astype(jnp.int32)
    return pltpu.make_async_copy(code_ref, scalar_ref, sem)


def slot_code(code_ref, d, k, query_len, queries):
    code = code_ref[d, query_len + k]
    return lax.div(code, jnp.int32(queries)), lax.rem(code, jnp.int32(queries))


def places(core, other, shape, queries):
    source = (1 - core) if other else core
    return iota(shape, 1) - queries * (source * shape[0] + iota(shape, 0))


def token_kernel(capacity, block, other, core_ref, recv_ref, emb_ref, *refs):
    if other:
        so_far_ref, *refs = refs
    extra_ref, token_ref, exp_ref, part_ref, *refs = refs
    both_ref, spots_ref, code_ref, acc_ref, scalar_ref, sem = refs
    chips, _, emb_dim = recv_ref.shape
    queries, query_len = block
    rows = queries * query_len
    core = core_ref[0]
    copy = unpack(core, recv_ref, rows, both_ref, spots_ref, extra_ref, code_ref, scalar_ref, sem)
    copy.start()
    acc_ref[...] = jnp.zeros_like(acc_ref)
    copy.wait()
    lane = iota((query_len, WIDE), 1).astype(F32)

    def one_group(group, carry):
        spots = picked(spots_ref, extra_ref, group, query_len, capacity)
        for step in range(GROUP):
            d = group * GROUP + step
            for k in range(capacity):
                p, j = slot_code(scalar_ref, d, k, query_len, queries)
                mask = jnp.where(spots[k][:, step : step + 1] == lane, 1.0, 0.0).astype(BF16)
                token = jnp.dot(mask, emb_ref[p], preferred_element_type=F32)
                token_ref[d, k] = token.astype(BF16)
                start = pl.multiple_of(j * query_len, query_len)
                query = recv_ref[d, pl.ds(start, query_len), :].astype(F32)
                acc_ref[k, pl.ds(d, 1), :] = jnp.sum(token * query, axis=0, keepdims=True)
        return carry

    lax.fori_loop(0, chips // GROUP, one_group, 0)
    shape = (chips, emb_dim)
    at = iota(shape, 1)
    extra = extra_ref[...]
    scores = jnp.zeros(shape, F32)
    for k in range(capacity):
        scores = jnp.where(at == k, jnp.sum(acc_ref[k], axis=-1, keepdims=True), scores)
    exps = jnp.where(at < capacity, jnp.exp(scores) * field(extra, query_len, VALID), 0.0)
    exp_ref[...] = exps
    which = field(extra, query_len, WHICH)
    place = places(core, other, shape, queries)
    total = jnp.zeros(shape, F32)
    for q in range(queries):
        share = jnp.sum(jnp.where(which == float(q), exps, 0.0), axis=1, keepdims=True)
        total = jnp.where(place == q, share, total)
    total = jnp.sum(total, axis=0, keepdims=True)
    if other:
        total = total + so_far_ref[0]
    part_ref[...] = jnp.broadcast_to(total[None], part_ref.shape)


def slot_weights(capacity, queries, query_len, neg, core, other, sums, extra, exps):
    place = places(core, other, exps.shape, queries)
    which = field(extra, query_len, WHICH)
    share = jnp.zeros_like(exps)
    for q in range(queries):
        norm = jnp.sum(jnp.where(place == q, sums, 0.0), axis=-1, keepdims=True)
        share = jnp.where(which == float(q), exps / norm, share)
    target = field(extra, query_len, HIGH) + field(extra, query_len, MID)
    target = target + field(extra, query_len, LOW)
    weights = neg * (share - target) * field(extra, query_len, VALID)
    return jnp.where(iota(exps.shape, 1) < capacity, weights, 0.0)


def weight_kernel(capacity, block, neg, other, core_ref, parts_ref, extra_ref, exp_ref, token_ref, out_ref, scale_ref):
    queries, query_len = block
    chips, emb_dim = exp_ref.shape
    extra = extra_ref[...]
    sums = jnp.sum(parts_ref[...], axis=0)
    weights = slot_weights(
        capacity, queries, query_len, neg, core_ref[0], other, sums, extra, exp_ref[...]
    )
    which = field(extra, query_len, WHICH)
    for q in range(queries):
        scale = jnp.where(which == float(q), weights, 0.0)
        for k in range(capacity):
            scale_ref[q * capacity + k] = jnp.broadcast_to(scale[:, k : k + 1], scale.shape)

    def one_device(d, carry):
        tokens = [token_ref[d, k].astype(F32) for k in range(capacity)]
        for q in range(queries):
            grad = scale_ref[q * capacity, pl.ds(d, 1), :] * tokens[0]
            for k in range(1, capacity):
                grad = grad + scale_ref[q * capacity + k, pl.ds(d, 1), :] * tokens[k]
            out_ref[d, q * query_len : (q + 1) * query_len, :] = grad.astype(BF16)
        return carry

    lax.fori_loop(0, chips, one_device, 0, unroll=8)


def add_kernel(left_ref, right_ref, out_ref):
    out_ref[...] = (left_ref[...].astype(F32) + right_ref[...].astype(F32)).astype(BF16)


def passage_kernel(capacity, block, neg, core_ref, hidden_ref, unit_ref, inverse_ref, parts_ref, *refs):
    halves = [refs[2 * h : 2 * h + 2] for h in range(CORES)]
    grad_ref, term_ref, table_ref, total_ref, weight_ref, *refs = refs[2 * CORES :]
    own_ref, unit_own_ref, inverse_own_ref, own_sem, *refs = refs
    loads = []
    for n, (source, target) in enumerate(
        ((hidden_ref, own_ref), (unit_ref, unit_own_ref), (inverse_ref, inverse_own_ref))
    ):
        loads.append(pltpu.make_async_copy(source, target, own_sem.at[n]))
        loads[n].start()
    passes, pass_len, _ = hidden_ref.shape
    emb_dim = unit_ref.shape[2]
    queries, query_len = block
    rows = queries * query_len
    lane = iota((query_len, WIDE), 1).astype(F32)
    copies = []
    for half, (recv_ref, _) in enumerate(halves):
        copy = unpack(core_ref[0], recv_ref, rows, *[ref.at[half] for ref in refs])
        copy.start()
        copies.append(copy)
    _, spots_ref, extra_ref, _, scalar_ref, _ = refs
    total_ref[...] = jnp.zeros_like(total_ref)
    table_ref[...] = jnp.zeros_like(table_ref)
    sums = jnp.sum(parts_ref[...], axis=0)
    for half, (recv_ref, exp_ref) in enumerate(halves):
        weights = slot_weights(
            capacity,
            queries,
            query_len,
            neg,
            core_ref[0],
            half == 1,
            sums,
            extra_ref[half],
            exp_ref[...],
        )
        for k in range(capacity):
            weight_ref[half, k] = jnp.broadcast_to(weights[:, k : k + 1], weights.shape)
    for half, (recv_ref, _) in enumerate(halves):
        chips = recv_ref.shape[0]
        copies[half].wait()

        def one_group(group, carry):
            spots = picked(spots_ref.at[half], extra_ref.at[half], group, query_len, capacity)

            def place(step, k):
                d = group * GROUP + step
                p, j = slot_code(scalar_ref.at[half], d, k, query_len, queries)
                return d, p, pl.multiple_of(step * rows + j * query_len, query_len)

            table_ref[...] = jnp.zeros_like(table_ref)
            for step in range(GROUP):
                for k in range(capacity):
                    d, p, start = place(step, k)
                    weight = weight_ref[half, k, pl.ds(d, 1), :]
                    weight = jnp.concatenate([weight] * (WIDE // emb_dim), axis=1)
                    added = jnp.where(spots[k][:, step : step + 1] == lane, weight, 0.0).astype(BF16)
                    table_ref[p, pl.ds(start, query_len), :] = (
                        table_ref[p, pl.ds(start, query_len), :] + added
                    )
            left = recv_ref[pl.ds(group * GROUP, GROUP), :rows, :].reshape(GROUP * rows, emb_dim)
            left = left.T
            for p in range(passes):
                total_ref[p] = total_ref[p] + jnp.dot(
                    left, table_ref[p], preferred_element_type=F32
                )
            return carry

        lax.fori_loop(0, chips // GROUP, one_group, 0)
    for load in loads:
        load.wait()
    term = jnp.zeros(term_ref.shape, F32)
    for p in range(passes):
        unit = unit_own_ref[p][:pass_len]
        grad = total_ref[p].T[:pass_len]
        grad = grad - unit * jnp.sum(unit * grad, axis=-1, keepdims=True)
        raw_grad = (grad * inverse_own_ref[p][:pass_len]).astype(BF16)
        grad_ref[p] = raw_grad
        term = term + lax.dot_general(
            raw_grad, own_ref[p], (((0,), (0,)), ((), ())), preferred_element_type=F32
        )
    term_ref[...] = term


def query_kernel(parts_ref, query_ref, proj_ref, term_ref, out_ref):
    hidden = query_ref[...]
    unit, length = unit_rows(jnp.dot(hidden, proj_ref[...], preferred_element_type=F32))
    grad = jnp.sum(parts_ref[...].astype(F32), axis=0)
    raw_grad = unit_back(grad, unit, length).astype(BF16)
    term = lax.dot_general(
        raw_grad, hidden, (((0,), (0,)), ((), ())), preferred_element_type=F32
    )
    term = term + term_ref[...]
    out_ref[...] = term.T.reshape(out_ref.shape).astype(BF16)


def swap(array, axes):
    return lax.all_to_all(array, axes, split_axis=0, concat_axis=0, tiled=True)


def to_other_core(array):
    return lax.ppermute(array, "core", [(c, CORES - 1 - c) for c in range(CORES)])


def per_device(query_hidden, passage_hidden, projection, negatives, positions, teacher):
    query_count, query_len, hidden_dim = query_hidden.shape
    pass_count, pass_len, _ = passage_hidden.shape
    emb_dim = projection.shape[1]
    neg_count = negatives.shape[1]
    chips = lax.axis_size("x") * lax.axis_size("z")
    owners = chips * CORES
    reps = lax.axis_size("rep")
    pair_count = query_count * neg_count
    capacity = (pair_count + owners - 2) // (owners - 1)
    rows = query_count * query_len
    block = (query_count, query_len)
    query_flat = query_hidden.reshape(rows, hidden_dim)
    core = lax.axis_index("core").reshape(1)

    def call(kernel, outs, scratch, *args, scalars=(), streamed=(), mb=16):
        results = pl.pallas_call(
            kernel,
            out_shape=outs,
            in_specs=[
                SMEM if n in scalars else pl.BlockSpec(memory_space=pl.ANY) if n in streamed else VMEM
                for n in range(len(args))
            ],
            out_specs=[VMEM] * len(outs),
            scratch_shapes=scratch,
            compiler_params=params(mb),
        )(*args)
        return results[0] if len(outs) == 1 else results

    shape = jax.ShapeDtypeStruct
    slot_shape = (chips, emb_dim)
    meta_shape = (chips, META_ROWS, emb_dim)
    recv_shape = (chips, rows + META_ROWS, emb_dim)
    send = call(
        lambda *refs: request_kernel(reps, pass_count, *refs),
        [shape(recv_shape, BF16)],
        [pltpu.VMEM(meta_shape, F32)],
        query_flat,
        projection,
        negatives,
        jnp.swapaxes(positions, 1, 2),
        teacher,
        mb=56,
    )
    near = swap(send, ("x", "z"))
    wide_shape = (pass_count, WIDE, emb_dim)
    emb, unit, inverse = call(
        embed_kernel,
        [shape(wide_shape, BF16), shape(wide_shape, F32), shape(wide_shape, F32)],
        [],
        passage_hidden,
        projection,
    )
    near, emb = lax.optimization_barrier((near, emb))
    far = to_other_core(near)
    halves = []
    so_far = []
    for other, recv in ((False, near), (True, far)):
        extra, tokens, exps, part = call(
            lambda *refs: token_kernel(capacity, block, other, *refs),
            [
                shape(slot_shape, F32),
                shape((chips, capacity, query_len, emb_dim), BF16),
                shape(slot_shape, F32),
                shape((owners if other else 1, 1, emb_dim), F32),
            ],
            [
                pltpu.VMEM(meta_shape, F32),
                pltpu.VMEM(slot_shape, F32),
                pltpu.VMEM(slot_shape, jnp.int32),
                pltpu.VMEM((capacity,) + slot_shape, F32),
                pltpu.SMEM(slot_shape, jnp.int32),
                pltpu.SemaphoreType.DMA,
            ],
            core,
            recv,
            emb,
            *so_far,
            scalars=(0,),
        )
        so_far = [part]
        halves.append((recv, extra, exps, tokens))
    parts = swap(part, ("x", "z", "core"))

    def weigh(other):
        _, extra, exps, tokens = halves[other]
        return call(
            lambda *refs: weight_kernel(capacity, block, neg_count, other, *refs),
            [shape((chips, rows, emb_dim), BF16)],
            [
                pltpu.VMEM((query_count * capacity,) + slot_shape, F32),
            ],
            core,
            parts,
            extra,
            exps,
            tokens,
            scalars=(0,),
        )

    far_part = to_other_core(weigh(True))
    near_part = weigh(False)
    query_parts = call(add_kernel, [shape(near_part.shape, BF16)], [], near_part, far_part)
    query_parts, sums = lax.optimization_barrier((query_parts, parts))
    query_parts = swap(query_parts, ("x", "z"))
    grad_passages, term = call(
        lambda *refs: passage_kernel(capacity, block, neg_count, *refs),
        [
            shape((pass_count, pass_len, emb_dim), BF16),
            shape((emb_dim, hidden_dim), F32),
        ],
        [
            pltpu.VMEM((pass_count, GROUP * rows, WIDE), BF16),
            pltpu.VMEM((pass_count, emb_dim, WIDE), F32),
        ]
        + [
            pltpu.VMEM((CORES, capacity) + slot_shape, F32),
            pltpu.VMEM(passage_hidden.shape, BF16),
            pltpu.VMEM(wide_shape, F32),
            pltpu.VMEM(wide_shape, F32),
            pltpu.SemaphoreType.DMA((3,)),
            pltpu.VMEM((CORES,) + meta_shape, F32),
            pltpu.VMEM((CORES,) + slot_shape, F32),
            pltpu.VMEM((CORES,) + slot_shape, F32),
            pltpu.VMEM((CORES,) + slot_shape, jnp.int32),
            pltpu.SMEM((CORES,) + slot_shape, jnp.int32),
            pltpu.SemaphoreType.DMA((CORES,)),
        ],
        core,
        passage_hidden,
        unit,
        inverse,
        sums,
        halves[0][0],
        halves[0][2],
        halves[1][0],
        halves[1][2],
        scalars=(0,),
        streamed=(1, 2, 3),
        mb=56,
    )
    groups = lax.axis_size(("x", "core", "rep"))
    pieces = call(
        query_kernel,
        [shape((groups, hidden_dim // groups, emb_dim), BF16)],
        [],
        query_parts,
        query_flat,
        projection,
        term,
        mb=16,
    )
    pieces = swap(pieces, ("x", "core", "rep"))
    mine = jnp.sum(pieces.astype(F32), axis=0).astype(BF16)
    copies = swap(jnp.broadcast_to(mine[None], (lax.axis_size("z"),) + mine.shape), "z")
    scale = 1.0 / math.sqrt(owners * reps * (query_count * query_len + pass_count * pass_len))
    mine = (jnp.sum(copies.astype(F32), axis=0) * scale).astype(BF16)
    copies = swap(jnp.broadcast_to(mine[None], (groups,) + mine.shape), ("x", "core", "rep"))
    return (grad_passages, copies.reshape(hidden_dim, emb_dim).astype(F32))


def solution(mesh):
    devices = mesh.devices.reshape(CHIPS_X, -1, CORES, mesh.shape["rep"])
    mesh = Mesh(devices, ("x", "z", "core", "rep"))
    whole = ("x", "z", "core", "rep")
    in_specs = (
        P(whole, None, None),
        P(whole, None, None),
        P(),
        P(whole, None),
        P(whole, None, None),
        P(whole, None),
    )
    out_specs = (P(whole, None, None), P())
    return jax.shard_map(
        per_device, mesh=mesh, in_specs=in_specs, out_specs=out_specs, check_vma=False
    )
```

```python
import math

import jax
import jax.numpy as jnp
from jax import lax
from jax.experimental import pallas as pl
from jax.experimental.pallas import tpu as pltpu
from jax.sharding import Mesh, PartitionSpec as P

F32 = jnp.float32
BF16 = jnp.bfloat16
CORES = 2
CHIPS_X = 4
SLOTS = 8
META_ROWS = 8
PER_CORE = 2
CODE, WHICH, VALID, HIGH, MID, LOW = range(6)
WIDE = 256
GROUP = 16
VMEM = pl.BlockSpec(memory_space=pltpu.VMEM)
SMEM = pl.BlockSpec(memory_space=pltpu.SMEM)


def params(mb):
    return pltpu.CompilerParams(vmem_limit_bytes=mb * 1024 * 1024)


def unit_rows(raw):
    length = jnp.sqrt(jnp.sum(raw * raw, axis=-1, keepdims=True) + 1e-06)
    return (raw / length, length)


def unit_back(grad, unit, length):
    return (grad - unit * jnp.sum(unit * grad, axis=-1, keepdims=True)) / length


def iota(shape, dim):
    return lax.broadcasted_iota(jnp.int32, shape, dim)


def request_kernel(reps, passes, query_ref, proj_ref, neg_ref, pos_ref, teacher_ref, send_ref, meta_ref):
    chips, _, emb_dim = send_ref.shape
    owners = chips * CORES
    queries, neg = neg_ref.shape
    query_len = pos_ref.shape[1]
    per_row = emb_dim // query_len
    unit, _ = unit_rows(jnp.dot(query_ref[...], proj_ref[...], preferred_element_type=F32))
    emb = unit.astype(BF16)
    send_ref[:, : emb.shape[0], :] = jnp.broadcast_to(emb[None], (chips,) + emb.shape)
    target = jnp.exp(teacher_ref[...])
    target = target / jnp.sum(target, axis=-1, keepdims=True)
    high = target.astype(BF16).astype(F32)
    rest = target - high
    mid = rest.astype(BF16).astype(F32)
    low = (rest - mid).astype(BF16).astype(F32)
    ids = neg_ref[...]
    owner = lax.div(ids, jnp.int32(reps * passes))
    within = lax.rem(ids, jnp.int32(passes))
    before = (iota((neg, neg), 0) < iota((neg, neg), 1)).astype(F32).astype(BF16)
    total = jnp.zeros((owners, 1), F32)
    meta = [jnp.zeros((chips, PER_CORE * emb_dim), F32) for _ in range(CORES)]
    for q in range(queries):
        mine = owner[q : q + 1, :]
        own = jnp.where(iota((owners, neg), 0) == mine, 1.0, 0.0)
        rank = jnp.dot(own.astype(BF16), before, preferred_element_type=F32) + total
        total = total + jnp.sum(own, axis=1, keepdims=True)
        rank = jnp.sum(own * rank, axis=0, keepdims=True).astype(jnp.int32)
        spots = pos_ref[q].astype(F32)
        lines = [jnp.where(rank == k, spots, 0.0) for k in range(per_row + 1)]
        values = {
            CODE: (within[q : q + 1, :] * queries + q).astype(F32),
            WHICH: jnp.full((1, neg), float(q), F32),
            VALID: jnp.ones((1, neg), F32),
            HIGH: high[q : q + 1, :],
            MID: mid[q : q + 1, :],
            LOW: low[q : q + 1, :],
        }
        line = iota((SLOTS, neg), 0)
        lines += [jnp.where(line == rank, values[at], 0.0) for at in sorted(values)]
        lines = jnp.concatenate(lines, axis=0)
        extra = PER_CORE * emb_dim - lines.shape[0]
        lines = jnp.concatenate([lines, jnp.zeros((extra, neg), F32)], axis=0)
        fields = jnp.concatenate([lines[:emb_dim].T, lines[emb_dim:].T], axis=1).astype(BF16)
        for c in range(CORES):
            to = jnp.where(iota((chips, neg), 0) * CORES + c == mine, 1.0, 0.0).astype(BF16)
            meta[c] = meta[c] + jnp.dot(to, fields, preferred_element_type=F32)
    meta_ref[...] = jnp.zeros_like(meta_ref)
    for c in range(CORES):
        for r in range(PER_CORE):
            meta_ref[:, c * PER_CORE + r, :] = meta[c][:, r * emb_dim : (r + 1) * emb_dim]
    send_ref[:, emb.shape[0] :, :] = meta_ref[...].astype(BF16)


def embed_kernel(hidden_ref, proj_ref, emb_ref, unit_ref, inverse_ref):
    passes, pass_len, _ = hidden_ref.shape
    unit_ref[...] = jnp.zeros_like(unit_ref)
    for p in range(passes):
        unit, length = unit_rows(jnp.dot(hidden_ref[p], proj_ref[...], preferred_element_type=F32))
        unit_ref[p, :pass_len, :] = unit
        inverse_ref[p, :pass_len, :] = jnp.broadcast_to(1.0 / length, unit.shape)
        emb_ref[p] = unit_ref[p].astype(BF16)


def field(extra, query_len, name):
    lanes = extra.shape[1]
    return pltpu.roll(extra, lanes - query_len - name * SLOTS, 1)


def picked(spots_ref, extra_ref, group, query_len, capacity):
    spots = spots_ref[pl.ds(pl.multiple_of(group * GROUP, GROUP), GROUP), :].T
    extra = extra_ref[pl.ds(pl.multiple_of(group * GROUP, GROUP), GROUP), :].T
    both = jnp.concatenate([spots, extra[:query_len]], axis=0)
    return [both[k * query_len : (k + 1) * query_len] for k in range(capacity)]


def unpack(core, recv_ref, rows, both_ref, spots_ref, extra_ref, code_ref, scalar_ref, sem):
    both_ref[...] = recv_ref[:, rows:, :].astype(F32)
    spots_ref[...] = jnp.where(core == 0, both_ref[:, 0, :], both_ref[:, PER_CORE, :])
    extra = jnp.where(core == 0, both_ref[:, 1, :], both_ref[:, PER_CORE + 1, :])
    extra_ref[...] = extra
    code_ref[...] = extra.astype(jnp.int32)
    return pltpu.make_async_copy(code_ref, scalar_ref, sem)


def slot_code(code_ref, d, k, query_len, queries):
    code = code_ref[d, query_len + k]
    return lax.div(code, jnp.int32(queries)), lax.rem(code, jnp.int32(queries))


def places(core, other, shape, queries):
    source = (1 - core) if other else core
    return iota(shape, 1) - queries * (source * shape[0] + iota(shape, 0))


def token_kernel(capacity, block, other, core_ref, recv_ref, emb_ref, *refs):
    if other:
        so_far_ref, near_ref, *refs = refs
    extra_ref, token_ref, exp_ref, part_ref, *refs = refs
    if other:
        kept_ref, *refs, keep_sem = refs
        keeps = []
        for n, source in enumerate((near_ref, recv_ref)):
            keeps.append(pltpu.make_async_copy(source, kept_ref.at[n], keep_sem.at[n]))
            keeps[n].start()
    both_ref, spots_ref, code_ref, acc_ref, scalar_ref, sem = refs
    chips, _, emb_dim = recv_ref.shape
    queries, query_len = block
    rows = queries * query_len
    core = core_ref[0]
    copy = unpack(core, recv_ref, rows, both_ref, spots_ref, extra_ref, code_ref, scalar_ref, sem)
    copy.start()
    acc_ref[...] = jnp.zeros_like(acc_ref)
    copy.wait()
    lane = iota((query_len, WIDE), 1).astype(F32)

    def one_group(group, carry):
        spots = picked(spots_ref, extra_ref, group, query_len, capacity)
        for step in range(GROUP):
            d = group * GROUP + step
            for k in range(capacity):
                p, j = slot_code(scalar_ref, d, k, query_len, queries)
                mask = jnp.where(spots[k][:, step : step + 1] == lane, 1.0, 0.0).astype(BF16)
                token = jnp.dot(mask, emb_ref[p], preferred_element_type=F32)
                token_ref[d, k] = token.astype(BF16)
                start = pl.multiple_of(j * query_len, query_len)
                query = recv_ref[d, pl.ds(start, query_len), :].astype(F32)
                acc_ref[k, pl.ds(d, 1), :] = jnp.sum(token * query, axis=0, keepdims=True)
        return carry

    lax.fori_loop(0, chips // GROUP, one_group, 0)
    shape = (chips, emb_dim)
    at = iota(shape, 1)
    extra = extra_ref[...]
    scores = jnp.zeros(shape, F32)
    for k in range(capacity):
        scores = jnp.where(at == k, jnp.sum(acc_ref[k], axis=-1, keepdims=True), scores)
    exps = jnp.where(at < capacity, jnp.exp(scores) * field(extra, query_len, VALID), 0.0)
    exp_ref[...] = exps
    which = field(extra, query_len, WHICH)
    place = places(core, other, shape, queries)
    total = jnp.zeros(shape, F32)
    for q in range(queries):
        share = jnp.sum(jnp.where(which == float(q), exps, 0.0), axis=1, keepdims=True)
        total = jnp.where(place == q, share, total)
    total = jnp.sum(total, axis=0, keepdims=True)
    if other:
        total = total + so_far_ref[0]
    part_ref[...] = jnp.broadcast_to(total[None], part_ref.shape)
    if other:
        for keep in keeps:
            keep.wait()


def slot_weights(capacity, queries, query_len, neg, core, other, sums, extra, exps):
    place = places(core, other, exps.shape, queries)
    which = field(extra, query_len, WHICH)
    share = jnp.zeros_like(exps)
    for q in range(queries):
        norm = jnp.sum(jnp.where(place == q, sums, 0.0), axis=-1, keepdims=True)
        share = jnp.where(which == float(q), exps / norm, share)
    target = field(extra, query_len, HIGH) + field(extra, query_len, MID)
    target = target + field(extra, query_len, LOW)
    weights = neg * (share - target) * field(extra, query_len, VALID)
    return jnp.where(iota(exps.shape, 1) < capacity, weights, 0.0)


def weight_kernel(capacity, block, neg, other, core_ref, parts_ref, extra_ref, exp_ref, token_ref, out_ref, scale_ref):
    queries, query_len = block
    chips, emb_dim = exp_ref.shape
    extra = extra_ref[...]
    sums = jnp.sum(parts_ref[...], axis=0)
    weights = slot_weights(
        capacity, queries, query_len, neg, core_ref[0], other, sums, extra, exp_ref[...]
    )
    which = field(extra, query_len, WHICH)
    for q in range(queries):
        scale = jnp.where(which == float(q), weights, 0.0)
        for k in range(capacity):
            scale_ref[q * capacity + k] = jnp.broadcast_to(scale[:, k : k + 1], scale.shape)

    def one_device(d, carry):
        tokens = [token_ref[d, k].astype(F32) for k in range(capacity)]
        for q in range(queries):
            grad = scale_ref[q * capacity, pl.ds(d, 1), :] * tokens[0]
            for k in range(1, capacity):
                grad = grad + scale_ref[q * capacity + k, pl.ds(d, 1), :] * tokens[k]
            out_ref[d, q * query_len : (q + 1) * query_len, :] = grad.astype(BF16)
        return carry

    lax.fori_loop(0, chips, one_device, 0, unroll=8)


def add_kernel(left_ref, right_ref, out_ref):
    out_ref[...] = (left_ref[...].astype(F32) + right_ref[...].astype(F32)).astype(BF16)


def passage_kernel(capacity, block, neg, core_ref, hidden_ref, unit_ref, inverse_ref, parts_ref, *refs):
    kept_ref, *refs = refs
    halves = [(kept_ref.at[h], refs[h]) for h in range(CORES)]
    grad_ref, term_ref, table_ref, total_ref, weight_ref, *refs = refs[CORES:]
    order_ref, own_ref, unit_own_ref, inverse_own_ref, own_sem, *refs = refs
    loads = []
    for n, (source, target) in enumerate(
        ((hidden_ref, own_ref), (unit_ref, unit_own_ref), (inverse_ref, inverse_own_ref))
    ):
        loads.append(pltpu.make_async_copy(source, target, own_sem.at[n]))
        loads[n].start()
    passes, pass_len, _ = hidden_ref.shape
    emb_dim = unit_ref.shape[2]
    queries, query_len = block
    rows = queries * query_len
    lane = iota((query_len, WIDE), 1).astype(F32)
    copies = []
    for half, (recv_ref, _) in enumerate(halves):
        copy = unpack(core_ref[0], recv_ref, rows, *[ref.at[half] for ref in refs])
        copy.start()
        copies.append(copy)
    _, spots_ref, extra_ref, _, scalar_ref, _ = refs
    total_ref[...] = jnp.zeros_like(total_ref)
    table_ref[...] = jnp.zeros_like(table_ref)
    sums = jnp.sum(parts_ref[...], axis=0)
    for half, (recv_ref, exp_ref) in enumerate(halves):
        weights = slot_weights(
            capacity,
            queries,
            query_len,
            neg,
            core_ref[0],
            half == 1,
            sums,
            extra_ref[half],
            exp_ref[...],
        )
        for k in range(capacity):
            weight_ref[half, k] = jnp.broadcast_to(weights[:, k : k + 1], weights.shape)
    for half, (recv_ref, _) in enumerate(halves):
        chips = recv_ref.shape[0]
        copies[half].wait()

        def one_group(group, carry):
            spots = picked(spots_ref.at[half], extra_ref.at[half], group, query_len, capacity)

            def place(step, k):
                d = group * GROUP + step
                p, j = slot_code(scalar_ref.at[half], d, k, query_len, queries)
                return d, p, pl.multiple_of(step * rows + j * query_len, query_len)

            table_ref[...] = jnp.zeros_like(table_ref)
            for step in range(GROUP):
                for k in range(capacity):
                    d, p, start = place(step, k)
                    weight = weight_ref[half, k, pl.ds(d, 1), :]
                    weight = jnp.concatenate([weight] * (WIDE // emb_dim), axis=1)
                    added = jnp.where(spots[k][:, step : step + 1] == lane, weight, 0.0).astype(BF16)
                    table_ref[p, pl.ds(start, query_len), :] = (
                        table_ref[p, pl.ds(start, query_len), :] + added
                    )
            left = recv_ref[pl.ds(group * GROUP, GROUP), :rows, :].reshape(GROUP * rows, emb_dim)
            left = left.T
            for p in range(passes):
                total_ref[p] = total_ref[p] + jnp.dot(
                    left, table_ref[p], preferred_element_type=F32
                )
            return carry

        lax.fori_loop(0, chips // GROUP, one_group, 0)
    for load in loads:
        load.wait()
    term = jnp.zeros(term_ref.shape, F32)
    for p in range(passes):
        unit = unit_own_ref[p][:pass_len]
        grad = total_ref[p].T[:pass_len]
        grad = grad - unit * jnp.sum(unit * grad, axis=-1, keepdims=True)
        raw_grad = (grad * inverse_own_ref[p][:pass_len]).astype(BF16)
        order_ref[:, p, :] = raw_grad.astype(F32)
        term = term + lax.dot_general(
            raw_grad, own_ref[p], (((0,), (0,)), ((), ())), preferred_element_type=F32
        )
    term_ref[...] = term
    grad_ref[...] = order_ref[...].astype(BF16)


def copy_kernel(from_ref, to_ref):
    to_ref[...] = from_ref[...]


def query_kernel(parts_ref, query_ref, proj_ref, term_ref, out_ref):
    hidden = query_ref[...]
    unit, length = unit_rows(jnp.dot(hidden, proj_ref[...], preferred_element_type=F32))
    grad = jnp.sum(parts_ref[...].astype(F32), axis=0)
    raw_grad = unit_back(grad, unit, length).astype(BF16)
    term = lax.dot_general(
        raw_grad, hidden, (((0,), (0,)), ((), ())), preferred_element_type=F32
    )
    term = term + term_ref[...]
    out_ref[...] = term.T.reshape(out_ref.shape).astype(BF16)


def swap(array, axes):
    return lax.all_to_all(array, axes, split_axis=0, concat_axis=0, tiled=True)


def to_other_core(array):
    return lax.ppermute(array, "core", [(c, CORES - 1 - c) for c in range(CORES)])


def per_device(query_hidden, passage_hidden, projection, negatives, positions, teacher):
    query_count, query_len, hidden_dim = query_hidden.shape
    pass_count, pass_len, _ = passage_hidden.shape
    emb_dim = projection.shape[1]
    neg_count = negatives.shape[1]
    chips = lax.axis_size("x") * lax.axis_size("z")
    owners = chips * CORES
    reps = lax.axis_size("rep")
    pair_count = query_count * neg_count
    capacity = (pair_count + owners - 2) // (owners - 1)
    rows = query_count * query_len
    block = (query_count, query_len)
    query_flat = query_hidden.reshape(rows, hidden_dim)
    core = lax.axis_index("core").reshape(1)

    def call(kernel, outs, scratch, *args, scalars=(), streamed=(), mb=16):
        results = pl.pallas_call(
            kernel,
            out_shape=outs,
            in_specs=[
                SMEM if n in scalars else pl.BlockSpec(memory_space=pl.ANY) if n in streamed else VMEM
                for n in range(len(args))
            ],
            out_specs=[VMEM] * len(outs),
            scratch_shapes=scratch,
            compiler_params=params(mb),
        )(*args)
        return results[0] if len(outs) == 1 else results

    shape = jax.ShapeDtypeStruct
    slot_shape = (chips, emb_dim)
    meta_shape = (chips, META_ROWS, emb_dim)
    recv_shape = (chips, rows + META_ROWS, emb_dim)
    send = call(
        lambda *refs: request_kernel(reps, pass_count, *refs),
        [shape(recv_shape, BF16)],
        [pltpu.VMEM(meta_shape, F32)],
        query_flat,
        projection,
        negatives,
        jnp.swapaxes(positions, 1, 2),
        teacher,
        mb=56,
    )
    near = swap(send, ("x", "z"))
    wide_shape = (pass_count, WIDE, emb_dim)
    emb, unit, inverse = call(
        embed_kernel,
        [shape(wide_shape, BF16), shape(wide_shape, F32), shape(wide_shape, F32)],
        [],
        passage_hidden,
        projection,
    )
    near, emb = lax.optimization_barrier((near, emb))
    far = to_other_core(near)
    halves = []
    so_far = []
    for other, recv in ((False, near), (True, far)):
        extra, tokens, exps, part, *kept = call(
            lambda *refs: token_kernel(capacity, block, other, *refs),
            [
                shape(slot_shape, F32),
                shape((chips, capacity, query_len, emb_dim), BF16),
                shape(slot_shape, F32),
                shape((owners if other else 1, 1, emb_dim), F32),
            ]
            + [shape((CORES,) + recv_shape, BF16)] * other,
            [
                pltpu.VMEM(meta_shape, F32),
                pltpu.VMEM(slot_shape, F32),
                pltpu.VMEM(slot_shape, jnp.int32),
                pltpu.VMEM((capacity,) + slot_shape, F32),
                pltpu.SMEM(slot_shape, jnp.int32),
                pltpu.SemaphoreType.DMA,
            ]
            + [pltpu.SemaphoreType.DMA((CORES,))] * other,
            core,
            recv,
            emb,
            *so_far,
            scalars=(0,),
        )
        so_far = [part, near]
        halves.append((extra, exps, tokens))
    parts = swap(part, ("x", "z", "core"))

    def weigh(other):
        extra, exps, tokens = halves[other]
        return call(
            lambda *refs: weight_kernel(capacity, block, neg_count, other, *refs),
            [shape((chips, rows, emb_dim), BF16)],
            [
                pltpu.VMEM((query_count * capacity,) + slot_shape, F32),
            ],
            core,
            parts,
            extra,
            exps,
            tokens,
            scalars=(0,),
        )

    far_part = to_other_core(weigh(True))
    near_part = weigh(False)
    query_parts = call(add_kernel, [shape(near_part.shape, BF16)], [], near_part, far_part)
    query_parts, sums = lax.optimization_barrier((query_parts, parts))
    query_parts = swap(query_parts, ("x", "z"))
    grad_passages, term = call(
        lambda *refs: passage_kernel(capacity, block, neg_count, *refs),
        [
            shape((pass_len, pass_count, emb_dim), BF16),
            shape((emb_dim, hidden_dim), F32),
        ],
        [
            pltpu.VMEM((pass_count, GROUP * rows, WIDE), BF16),
            pltpu.VMEM((pass_count, emb_dim, WIDE), F32),
        ]
        + [
            pltpu.VMEM((CORES, capacity) + slot_shape, F32),
            pltpu.VMEM((pass_len, pass_count, emb_dim), F32),
            pltpu.VMEM(passage_hidden.shape, BF16),
            pltpu.VMEM(wide_shape, F32),
            pltpu.VMEM(wide_shape, F32),
            pltpu.SemaphoreType.DMA((3,)),
            pltpu.VMEM((CORES,) + meta_shape, F32),
            pltpu.VMEM((CORES,) + slot_shape, F32),
            pltpu.VMEM((CORES,) + slot_shape, F32),
            pltpu.VMEM((CORES,) + slot_shape, jnp.int32),
            pltpu.SMEM((CORES,) + slot_shape, jnp.int32),
            pltpu.SemaphoreType.DMA((CORES,)),
        ],
        core,
        passage_hidden,
        unit,
        inverse,
        sums,
        kept[0],
        halves[0][1],
        halves[1][1],
        scalars=(0,),
        streamed=(1, 2, 3),
        mb=56,
    )
    term = call(copy_kernel, [shape(term.shape, F32)], [], term, mb=8)
    groups = lax.axis_size(("x", "core", "rep"))
    pieces = call(
        query_kernel,
        [shape((groups, hidden_dim // groups, emb_dim), BF16)],
        [],
        query_parts,
        query_flat,
        projection,
        term,
        mb=16,
    )
    pieces = swap(pieces, ("x", "core", "rep"))
    mine = jnp.sum(pieces.astype(F32), axis=0).astype(BF16)
    copies = swap(jnp.broadcast_to(mine[None], (lax.axis_size("z"),) + mine.shape), "z")
    scale = 1.0 / math.sqrt(owners * reps * (query_count * query_len + pass_count * pass_len))
    mine = (jnp.sum(copies.astype(F32), axis=0) * scale).astype(BF16)
    copies = swap(jnp.broadcast_to(mine[None], (groups,) + mine.shape), ("x", "core", "rep"))
    grad_passages = jnp.swapaxes(grad_passages, 0, 1)
    return (grad_passages, copies.reshape(hidden_dim, emb_dim).astype(F32))


def solution(mesh):
    devices = mesh.devices.reshape(CHIPS_X, -1, CORES, mesh.shape["rep"])
    mesh = Mesh(devices, ("x", "z", "core", "rep"))
    whole = ("x", "z", "core", "rep")
    in_specs = (
        P(whole, None, None),
        P(whole, None, None),
        P(),
        P(whole, None),
        P(whole, None, None),
        P(whole, None),
    )
    out_specs = (P(whole, None, None), P())
    return jax.shard_map(
        per_device, mesh=mesh, in_specs=in_specs, out_specs=out_specs, check_vma=False
    )
```

```python
import math

import jax
import jax.numpy as jnp
from jax import lax
from jax.experimental import pallas as pl
from jax.experimental.pallas import tpu as pltpu
from jax.sharding import Mesh, PartitionSpec as P

F32 = jnp.float32
BF16 = jnp.bfloat16
CORES = 2
CHIPS_X = 4
SLOTS = 8
META_ROWS = 8
PER_CORE = 2
CODE, WHICH, VALID, HIGH, MID, LOW = range(6)
WIDE = 256
GROUP = 16
VMEM = pl.BlockSpec(memory_space=pltpu.VMEM)
SMEM = pl.BlockSpec(memory_space=pltpu.SMEM)


def params(mb):
    return pltpu.CompilerParams(vmem_limit_bytes=mb * 1024 * 1024)


def unit_rows(raw):
    length = jnp.sqrt(jnp.sum(raw * raw, axis=-1, keepdims=True) + 1e-06)
    return (raw / length, length)


def unit_back(grad, unit, length):
    return (grad - unit * jnp.sum(unit * grad, axis=-1, keepdims=True)) / length


def iota(shape, dim):
    return lax.broadcasted_iota(jnp.int32, shape, dim)


def request_kernel(reps, passes, query_ref, proj_ref, neg_ref, pos_ref, teacher_ref, send_ref, meta_ref):
    chips, _, emb_dim = send_ref.shape
    owners = chips * CORES
    queries, neg = neg_ref.shape
    query_len = pos_ref.shape[1]
    per_row = emb_dim // query_len
    unit, _ = unit_rows(jnp.dot(query_ref[...], proj_ref[...], preferred_element_type=F32))
    target = jnp.exp(teacher_ref[...])
    target = target / jnp.sum(target, axis=-1, keepdims=True)
    high = target.astype(BF16).astype(F32)
    rest = target - high
    mid = rest.astype(BF16).astype(F32)
    low = (rest - mid).astype(BF16).astype(F32)
    ids = neg_ref[...]
    owner = lax.div(ids, jnp.int32(reps * passes))
    within = lax.rem(ids, jnp.int32(passes))
    before = (iota((neg, neg), 0) < iota((neg, neg), 1)).astype(F32).astype(BF16)
    total = jnp.zeros((owners, 1), F32)
    meta = [jnp.zeros((chips, PER_CORE * emb_dim), F32) for _ in range(CORES)]
    for q in range(queries):
        mine = owner[q : q + 1, :]
        own = jnp.where(iota((owners, neg), 0) == mine, 1.0, 0.0)
        rank = jnp.dot(own.astype(BF16), before, preferred_element_type=F32) + total
        total = total + jnp.sum(own, axis=1, keepdims=True)
        rank = jnp.sum(own * rank, axis=0, keepdims=True).astype(jnp.int32)
        spots = pos_ref[q].astype(F32)
        lines = [jnp.where(rank == k, spots, 0.0) for k in range(per_row + 1)]
        values = {
            CODE: (within[q : q + 1, :] * queries + q).astype(F32),
            WHICH: jnp.full((1, neg), float(q), F32),
            VALID: jnp.ones((1, neg), F32),
            HIGH: high[q : q + 1, :],
            MID: mid[q : q + 1, :],
            LOW: low[q : q + 1, :],
        }
        line = iota((SLOTS, neg), 0)
        lines += [jnp.where(line == rank, values[at], 0.0) for at in sorted(values)]
        lines = jnp.concatenate(lines, axis=0)
        extra = PER_CORE * emb_dim - lines.shape[0]
        lines = jnp.concatenate([lines, jnp.zeros((extra, neg), F32)], axis=0)
        fields = jnp.concatenate([lines[:emb_dim].T, lines[emb_dim:].T], axis=1).astype(BF16)
        for c in range(CORES):
            to = jnp.where(iota((chips, neg), 0) * CORES + c == mine, 1.0, 0.0).astype(BF16)
            meta[c] = meta[c] + jnp.dot(to, fields, preferred_element_type=F32)
    meta_ref[...] = jnp.zeros_like(meta_ref)
    for c in range(CORES):
        for r in range(PER_CORE):
            meta_ref[:, c * PER_CORE + r, :] = meta[c][:, r * emb_dim : (r + 1) * emb_dim]
    wide = jnp.broadcast_to(unit[None], (chips,) + unit.shape)
    send_ref[...] = jnp.concatenate([wide, meta_ref[...]], axis=1).astype(BF16)


def embed_kernel(hidden_ref, proj_ref, emb_ref, unit_ref, inverse_ref):
    passes, pass_len, _ = hidden_ref.shape
    unit_ref[...] = jnp.zeros_like(unit_ref)
    for p in range(passes):
        unit, length = unit_rows(jnp.dot(hidden_ref[p], proj_ref[...], preferred_element_type=F32))
        unit_ref[p, :pass_len, :] = unit
        inverse_ref[p, :pass_len, :] = jnp.broadcast_to(1.0 / length, unit.shape)
        emb_ref[p] = unit_ref[p].astype(BF16)


def field(extra, query_len, name):
    lanes = extra.shape[1]
    return pltpu.roll(extra, lanes - query_len - name * SLOTS, 1)


def picked(spots_ref, extra_ref, group, query_len, capacity, size=GROUP):
    spots = spots_ref[pl.ds(pl.multiple_of(group * size, size), size), :].T
    extra = extra_ref[pl.ds(pl.multiple_of(group * size, size), size), :].T
    both = jnp.concatenate([spots, extra[:query_len]], axis=0)
    return [both[k * query_len : (k + 1) * query_len] for k in range(capacity)]


def unpack(core, recv_ref, rows, both_ref, spots_ref, extra_ref, code_ref, scalar_ref, sem):
    both_ref[...] = recv_ref[...].astype(F32)[:, rows:, :]
    spots_ref[...] = jnp.where(core == 0, both_ref[:, 0, :], both_ref[:, PER_CORE, :])
    extra = jnp.where(core == 0, both_ref[:, 1, :], both_ref[:, PER_CORE + 1, :])
    extra_ref[...] = extra
    code_ref[...] = extra.astype(jnp.int32)
    return pltpu.make_async_copy(code_ref, scalar_ref, sem)


def slot_code(code_ref, d, k, query_len, queries):
    code = code_ref[d, query_len + k]
    return lax.div(code, jnp.int32(queries)), lax.rem(code, jnp.int32(queries))


def places(core, other, shape, queries):
    source = (1 - core) if other else core
    return iota(shape, 1) - queries * (source * shape[0] + iota(shape, 0))


def token_kernel(capacity, block, other, core_ref, recv_ref, emb_ref, *refs):
    if other:
        so_far_ref, near_ref, *refs = refs
    extra_ref, token_ref, exp_ref, part_ref, *refs = refs
    if other:
        kept_ref, *refs = refs
        kept_ref[0] = near_ref[...]
        kept_ref[1] = recv_ref[...]
    both_ref, spots_ref, code_ref, acc_ref, scalar_ref, sem = refs
    chips, _, emb_dim = recv_ref.shape
    queries, query_len = block
    rows = queries * query_len
    core = core_ref[0]
    copy = unpack(core, recv_ref, rows, both_ref, spots_ref, extra_ref, code_ref, scalar_ref, sem)
    copy.start()
    acc_ref[...] = jnp.zeros_like(acc_ref)
    copy.wait()
    lane = iota((query_len, WIDE), 1).astype(F32)

    spots = picked(spots_ref, extra_ref, 0, query_len, capacity, chips)
    for d in range(chips):
        for k in range(capacity):
            p, j = slot_code(scalar_ref, d, k, query_len, queries)
            mask = jnp.where(spots[k][:, d : d + 1] == lane, 1.0, 0.0).astype(BF16)
            token = jnp.dot(mask, emb_ref[p], preferred_element_type=F32)
            token_ref[d, k] = token.astype(BF16)
            start = pl.multiple_of(j * query_len, query_len)
            query = recv_ref[d, pl.ds(start, query_len), :].astype(F32)
            acc_ref[k, d : d + 1, :] = jnp.sum(token * query, axis=0, keepdims=True)
    shape = (chips, emb_dim)
    at = iota(shape, 1)
    extra = extra_ref[...]
    scores = jnp.zeros(shape, F32)
    for k in range(capacity):
        scores = jnp.where(at == k, jnp.sum(acc_ref[k], axis=-1, keepdims=True), scores)
    exps = jnp.where(at < capacity, jnp.exp(scores) * field(extra, query_len, VALID), 0.0)
    exp_ref[...] = exps
    which = field(extra, query_len, WHICH)
    place = places(core, other, shape, queries)
    total = jnp.zeros(shape, F32)
    for q in range(queries):
        share = jnp.sum(jnp.where(which == float(q), exps, 0.0), axis=1, keepdims=True)
        total = jnp.where(place == q, share, total)
    total = jnp.sum(total, axis=0, keepdims=True)
    if other:
        total = total + so_far_ref[0]
    part_ref[...] = jnp.broadcast_to(total[None], part_ref.shape)


def slot_weights(capacity, queries, query_len, neg, core, other, sums, extra, exps):
    place = places(core, other, exps.shape, queries)
    which = field(extra, query_len, WHICH)
    share = jnp.zeros_like(exps)
    for q in range(queries):
        norm = jnp.sum(jnp.where(place == q, sums, 0.0), axis=-1, keepdims=True)
        share = jnp.where(which == float(q), exps / norm, share)
    target = field(extra, query_len, HIGH) + field(extra, query_len, MID)
    target = target + field(extra, query_len, LOW)
    weights = neg * (share - target) * field(extra, query_len, VALID)
    return jnp.where(iota(exps.shape, 1) < capacity, weights, 0.0)


def weight_kernel(capacity, block, neg, other, core_ref, parts_ref, extra_ref, exp_ref, token_ref, out_ref, scale_ref):
    queries, query_len = block
    chips, emb_dim = exp_ref.shape
    extra = extra_ref[...]
    sums = jnp.sum(parts_ref[...], axis=0)
    weights = slot_weights(
        capacity, queries, query_len, neg, core_ref[0], other, sums, extra, exp_ref[...]
    )
    which = field(extra, query_len, WHICH)
    for q in range(queries):
        scale = jnp.where(which == float(q), weights, 0.0)
        for k in range(capacity):
            scale_ref[q * capacity + k] = jnp.broadcast_to(scale[:, k : k + 1], scale.shape)

    def one_device(d, carry):
        tokens = [token_ref[d, k].astype(F32) for k in range(capacity)]
        for q in range(queries):
            grad = scale_ref[q * capacity, pl.ds(d, 1), :] * tokens[0]
            for k in range(1, capacity):
                grad = grad + scale_ref[q * capacity + k, pl.ds(d, 1), :] * tokens[k]
            out_ref[d, q * query_len : (q + 1) * query_len, :] = grad.astype(BF16)
        return carry

    lax.fori_loop(0, chips, one_device, 0, unroll=8)


def add_kernel(left_ref, right_ref, out_ref):
    out_ref[...] = (left_ref[...].astype(F32) + right_ref[...].astype(F32)).astype(BF16)


def passage_kernel(capacity, block, neg, core_ref, hidden_ref, unit_ref, inverse_ref, parts_ref, *refs):
    kept_ref, *refs = refs
    halves = [(kept_ref.at[h], refs[h]) for h in range(CORES)]
    grad_ref, term_ref, table_ref, total_ref, weight_ref, *refs = refs[CORES:]
    order_ref, unit_own_ref, inverse_own_ref, own_sem, *refs = refs
    loads = []
    for n, (source, target) in enumerate(
        ((unit_ref, unit_own_ref), (inverse_ref, inverse_own_ref))
    ):
        loads.append(pltpu.make_async_copy(source, target, own_sem.at[n]))
        loads[n].start()
    passes, pass_len, _ = hidden_ref.shape
    emb_dim = unit_ref.shape[2]
    queries, query_len = block
    rows = queries * query_len
    lane = iota((query_len, WIDE), 1).astype(F32)
    copies = []
    for half, (recv_ref, _) in enumerate(halves):
        copy = unpack(core_ref[0], recv_ref, rows, *[ref.at[half] for ref in refs])
        copy.start()
        copies.append(copy)
    _, spots_ref, extra_ref, _, scalar_ref, _ = refs
    total_ref[...] = jnp.zeros_like(total_ref)
    table_ref[...] = jnp.zeros_like(table_ref)
    sums = jnp.sum(parts_ref[...], axis=0)
    for half, (recv_ref, exp_ref) in enumerate(halves):
        weights = slot_weights(
            capacity,
            queries,
            query_len,
            neg,
            core_ref[0],
            half == 1,
            sums,
            extra_ref[half],
            exp_ref[...],
        )
        for k in range(capacity):
            weight_ref[half, k] = jnp.broadcast_to(weights[:, k : k + 1], weights.shape)
    for half, (recv_ref, _) in enumerate(halves):
        chips = recv_ref.shape[0]
        copies[half].wait()

        def one_group(group, carry):
            spots = picked(spots_ref.at[half], extra_ref.at[half], group, query_len, capacity)

            def place(step, k):
                d = group * GROUP + step
                p, j = slot_code(scalar_ref.at[half], d, k, query_len, queries)
                return d, p, pl.multiple_of(step * rows + j * query_len, query_len)

            table_ref[...] = jnp.zeros_like(table_ref)
            for step in range(GROUP):
                for k in range(capacity):
                    d, p, start = place(step, k)
                    weight = weight_ref[half, k, pl.ds(d, 1), :]
                    weight = jnp.concatenate([weight] * (WIDE // emb_dim), axis=1)
                    added = jnp.where(spots[k][:, step : step + 1] == lane, weight, 0.0).astype(BF16)
                    table_ref[p, pl.ds(start, query_len), :] = (
                        table_ref[p, pl.ds(start, query_len), :] + added
                    )
            left = recv_ref[pl.ds(group * GROUP, GROUP), :rows, :].reshape(GROUP * rows, emb_dim)
            left = left.T
            for p in range(passes):
                total_ref[p] = total_ref[p] + jnp.dot(
                    left, table_ref[p], preferred_element_type=F32
                )
            return carry

        lax.fori_loop(0, chips // GROUP, one_group, 0)
    for load in loads:
        load.wait()
    term = jnp.zeros(term_ref.shape, F32)
    for p in range(passes):
        unit = unit_own_ref[p][:pass_len]
        grad = total_ref[p].T[:pass_len]
        grad = grad - unit * jnp.sum(unit * grad, axis=-1, keepdims=True)
        raw_grad = (grad * inverse_own_ref[p][:pass_len]).astype(BF16)
        order_ref[:, p, :] = raw_grad.astype(F32)
        term = term + lax.dot_general(
            raw_grad, hidden_ref[p], (((0,), (0,)), ((), ())), preferred_element_type=F32
        )
    term_ref[...] = term
    grad_ref[...] = order_ref[...].astype(BF16)


def copy_kernel(from_ref, to_ref):
    to_ref[...] = from_ref[...]


def query_kernel(parts_ref, query_ref, proj_ref, term_ref, out_ref):
    hidden = query_ref[...]
    unit, length = unit_rows(jnp.dot(hidden, proj_ref[...], preferred_element_type=F32))
    grad = jnp.sum(parts_ref[...].astype(F32), axis=0)
    raw_grad = unit_back(grad, unit, length).astype(BF16)
    term = lax.dot_general(
        raw_grad, hidden, (((0,), (0,)), ((), ())), preferred_element_type=F32
    )
    term = term + term_ref[...]
    out_ref[...] = term.T.reshape(out_ref.shape).astype(BF16)


def swap(array, axes):
    return lax.all_to_all(array, axes, split_axis=0, concat_axis=0, tiled=True)


def to_other_core(array):
    return lax.ppermute(array, "core", [(c, CORES - 1 - c) for c in range(CORES)])


def per_device(query_hidden, passage_hidden, projection, negatives, positions, teacher):
    query_count, query_len, hidden_dim = query_hidden.shape
    pass_count, pass_len, _ = passage_hidden.shape
    emb_dim = projection.shape[1]
    neg_count = negatives.shape[1]
    chips = lax.axis_size("x") * lax.axis_size("z")
    owners = chips * CORES
    reps = lax.axis_size("rep")
    pair_count = query_count * neg_count
    capacity = (pair_count + owners - 2) // (owners - 1)
    rows = query_count * query_len
    block = (query_count, query_len)
    query_flat = query_hidden.reshape(rows, hidden_dim)
    core = lax.axis_index("core").reshape(1)

    def call(kernel, outs, scratch, *args, scalars=(), streamed=(), mb=16):
        results = pl.pallas_call(
            kernel,
            out_shape=outs,
            in_specs=[
                SMEM if n in scalars else pl.BlockSpec(memory_space=pl.ANY) if n in streamed else VMEM
                for n in range(len(args))
            ],
            out_specs=[VMEM] * len(outs),
            scratch_shapes=scratch,
            compiler_params=params(mb),
        )(*args)
        return results[0] if len(outs) == 1 else results

    shape = jax.ShapeDtypeStruct
    slot_shape = (chips, emb_dim)
    meta_shape = (chips, META_ROWS, emb_dim)
    recv_shape = (chips, rows + META_ROWS, emb_dim)
    send = call(
        lambda *refs: request_kernel(reps, pass_count, *refs),
        [shape(recv_shape, BF16)],
        [pltpu.VMEM(meta_shape, F32)],
        query_flat,
        projection,
        negatives,
        jnp.swapaxes(positions, 1, 2),
        teacher,
        mb=56,
    )
    near = swap(send, ("x", "z"))
    wide_shape = (pass_count, WIDE, emb_dim)
    emb, unit, inverse = call(
        embed_kernel,
        [shape(wide_shape, BF16), shape(wide_shape, F32), shape(wide_shape, F32)],
        [],
        passage_hidden,
        projection,
    )
    near, emb = lax.optimization_barrier((near, emb))
    far = to_other_core(near)
    halves = []
    so_far = []
    for other, recv in ((False, near), (True, far)):
        extra, tokens, exps, part, *kept = call(
            lambda *refs: token_kernel(capacity, block, other, *refs),
            [
                shape(slot_shape, F32),
                shape((chips, capacity, query_len, emb_dim), BF16),
                shape(slot_shape, F32),
                shape((owners if other else 1, 1, emb_dim), F32),
            ]
            + [shape((CORES,) + recv_shape, BF16)] * other,
            [
                pltpu.VMEM(meta_shape, F32),
                pltpu.VMEM(slot_shape, F32),
                pltpu.VMEM(slot_shape, jnp.int32),
                pltpu.VMEM((capacity,) + slot_shape, F32),
                pltpu.SMEM(slot_shape, jnp.int32),
                pltpu.SemaphoreType.DMA,
            ],
            core,
            recv,
            emb,
            *so_far,
            scalars=(0,),
        )
        so_far = [part, near]
        halves.append((extra, exps, tokens))
    parts = swap(part, ("x", "z", "core"))

    def weigh(other):
        extra, exps, tokens = halves[other]
        return call(
            lambda *refs: weight_kernel(capacity, block, neg_count, other, *refs),
            [shape((chips, rows, emb_dim), BF16)],
            [
                pltpu.VMEM((query_count * capacity,) + slot_shape, F32),
            ],
            core,
            parts,
            extra,
            exps,
            tokens,
            scalars=(0,),
        )

    far_part = to_other_core(weigh(True))
    near_part = weigh(False)
    query_parts = call(add_kernel, [shape(near_part.shape, BF16)], [], near_part, far_part)
    query_parts, sums = lax.optimization_barrier((query_parts, parts))
    query_parts = swap(query_parts, ("x", "z"))
    grad_passages, term = call(
        lambda *refs: passage_kernel(capacity, block, neg_count, *refs),
        [
            shape((pass_len, pass_count, emb_dim), BF16),
            shape((emb_dim, hidden_dim), F32),
        ],
        [
            pltpu.VMEM((pass_count, GROUP * rows, WIDE), BF16),
            pltpu.VMEM((pass_count, emb_dim, WIDE), F32),
        ]
        + [
            pltpu.VMEM((CORES, capacity) + slot_shape, F32),
            pltpu.VMEM((pass_len, pass_count, emb_dim), F32),
            pltpu.VMEM(wide_shape, F32),
            pltpu.VMEM(wide_shape, F32),
            pltpu.SemaphoreType.DMA((2,)),
            pltpu.VMEM((CORES,) + meta_shape, F32),
            pltpu.VMEM((CORES,) + slot_shape, F32),
            pltpu.VMEM((CORES,) + slot_shape, F32),
            pltpu.VMEM((CORES,) + slot_shape, jnp.int32),
            pltpu.SMEM((CORES,) + slot_shape, jnp.int32),
            pltpu.SemaphoreType.DMA((CORES,)),
        ],
        core,
        passage_hidden,
        unit,
        inverse,
        sums,
        kept[0],
        halves[0][1],
        halves[1][1],
        scalars=(0,),
        streamed=(2, 3),
        mb=56,
    )
    term = call(copy_kernel, [shape(term.shape, F32)], [], term, mb=8)
    groups = lax.axis_size(("x", "core", "rep"))
    pieces = call(
        query_kernel,
        [shape((groups, hidden_dim // groups, emb_dim), BF16)],
        [],
        query_parts,
        query_flat,
        projection,
        term,
        mb=16,
    )
    pieces = swap(pieces, ("x", "core", "rep"))
    mine = jnp.sum(pieces.astype(F32), axis=0).astype(BF16)
    copies = swap(jnp.broadcast_to(mine[None], (lax.axis_size("z"),) + mine.shape), "z")
    scale = 1.0 / math.sqrt(owners * reps * (query_count * query_len + pass_count * pass_len))
    mine = (jnp.sum(copies.astype(F32), axis=0) * scale).astype(BF16)
    copies = swap(jnp.broadcast_to(mine[None], (groups,) + mine.shape), ("x", "core", "rep"))
    grad_passages = jnp.swapaxes(grad_passages, 0, 1)
    return (grad_passages, copies.reshape(hidden_dim, emb_dim).astype(F32))


def solution(mesh):
    devices = mesh.devices.reshape(CHIPS_X, -1, CORES, mesh.shape["rep"])
    mesh = Mesh(devices, ("x", "z", "core", "rep"))
    whole = ("x", "z", "core", "rep")
    in_specs = (
        P(whole, None, None),
        P(whole, None, None),
        P(),
        P(whole, None),
        P(whole, None, None),
        P(whole, None),
    )
    out_specs = (P(whole, None, None), P())
    return jax.shard_map(
        per_device, mesh=mesh, in_specs=in_specs, out_specs=out_specs, check_vma=False
    )
```

```python
import math

import jax
import jax.numpy as jnp
from jax import lax
from jax.experimental import pallas as pl
from jax.experimental.pallas import tpu as pltpu
from jax.sharding import Mesh, PartitionSpec as P

F32 = jnp.float32
BF16 = jnp.bfloat16
CORES = 2
CHIPS_X = 4
SLOTS = 8
META_ROWS = 8
PER_CORE = 2
CODE, WHICH, VALID, HIGH, MID, LOW = range(6)
WIDE = 256
GROUP = 16
VMEM = pl.BlockSpec(memory_space=pltpu.VMEM)
SMEM = pl.BlockSpec(memory_space=pltpu.SMEM)


def params(mb):
    return pltpu.CompilerParams(vmem_limit_bytes=mb * 1024 * 1024)


def unit_rows(raw):
    length = jnp.sqrt(jnp.sum(raw * raw, axis=-1, keepdims=True) + 1e-06)
    return (raw / length, length)


def unit_back(grad, unit, length):
    return (grad - unit * jnp.sum(unit * grad, axis=-1, keepdims=True)) / length


def iota(shape, dim):
    return lax.broadcasted_iota(jnp.int32, shape, dim)


def request_kernel(reps, passes, query_ref, proj_ref, neg_ref, pos_ref, teacher_ref, send_ref, meta_ref):
    chips, _, emb_dim = send_ref.shape
    owners = chips * CORES
    queries, neg = neg_ref.shape
    query_len = pos_ref.shape[1]
    per_row = emb_dim // query_len
    unit, _ = unit_rows(jnp.dot(query_ref[...], proj_ref[...], preferred_element_type=F32))
    target = jnp.exp(teacher_ref[...])
    target = target / jnp.sum(target, axis=-1, keepdims=True)
    high = target.astype(BF16).astype(F32)
    rest = target - high
    mid = rest.astype(BF16).astype(F32)
    low = (rest - mid).astype(BF16).astype(F32)
    ids = neg_ref[...]
    owner = lax.div(ids, jnp.int32(reps * passes))
    within = lax.rem(ids, jnp.int32(passes))
    before = (iota((neg, neg), 0) < iota((neg, neg), 1)).astype(F32).astype(BF16)
    total = jnp.zeros((owners, 1), F32)
    meta = [jnp.zeros((chips, PER_CORE * emb_dim), F32) for _ in range(CORES)]
    for q in range(queries):
        mine = owner[q : q + 1, :]
        own = jnp.where(iota((owners, neg), 0) == mine, 1.0, 0.0)
        rank = jnp.dot(own.astype(BF16), before, preferred_element_type=F32) + total
        total = total + jnp.sum(own, axis=1, keepdims=True)
        rank = jnp.sum(own * rank, axis=0, keepdims=True).astype(jnp.int32)
        spots = pos_ref[q].astype(F32)
        lines = [jnp.where(rank == k, spots, 0.0) for k in range(per_row + 1)]
        values = {
            CODE: (within[q : q + 1, :] * queries + q).astype(F32),
            WHICH: jnp.full((1, neg), float(q), F32),
            VALID: jnp.ones((1, neg), F32),
            HIGH: high[q : q + 1, :],
            MID: mid[q : q + 1, :],
            LOW: low[q : q + 1, :],
        }
        line = iota((SLOTS, neg), 0)
        lines += [jnp.where(line == rank, values[at], 0.0) for at in sorted(values)]
        lines = jnp.concatenate(lines, axis=0)
        extra = PER_CORE * emb_dim - lines.shape[0]
        lines = jnp.concatenate([lines, jnp.zeros((extra, neg), F32)], axis=0)
        fields = jnp.concatenate([lines[:emb_dim].T, lines[emb_dim:].T], axis=1).astype(BF16)
        for c in range(CORES):
            to = jnp.where(iota((chips, neg), 0) * CORES + c == mine, 1.0, 0.0).astype(BF16)
            meta[c] = meta[c] + jnp.dot(to, fields, preferred_element_type=F32)
    meta_ref[...] = jnp.zeros_like(meta_ref)
    for c in range(CORES):
        for r in range(PER_CORE):
            meta_ref[:, c * PER_CORE + r, :] = meta[c][:, r * emb_dim : (r + 1) * emb_dim]
    wide = jnp.broadcast_to(unit[None], (chips,) + unit.shape)
    send_ref[...] = jnp.concatenate([wide, meta_ref[...]], axis=1).astype(BF16)


def embed_kernel(hidden_ref, proj_ref, emb_ref, unit_ref, inverse_ref):
    passes, pass_len, _ = hidden_ref.shape
    unit_ref[...] = jnp.zeros_like(unit_ref)
    for p in range(passes):
        unit, length = unit_rows(jnp.dot(hidden_ref[p], proj_ref[...], preferred_element_type=F32))
        unit_ref[p, :pass_len, :] = unit
        inverse_ref[p, :pass_len, :] = jnp.broadcast_to(1.0 / length, unit.shape)
        emb_ref[p] = unit_ref[p].astype(BF16)


def field(extra, query_len, name):
    lanes = extra.shape[1]
    return pltpu.roll(extra, lanes - query_len - name * SLOTS, 1)


def picked(spots_ref, extra_ref, group, query_len, capacity, size=GROUP):
    spots = spots_ref[pl.ds(pl.multiple_of(group * size, size), size), :].T
    extra = extra_ref[pl.ds(pl.multiple_of(group * size, size), size), :].T
    both = jnp.concatenate([spots, extra[:query_len]], axis=0)
    return [both[k * query_len : (k + 1) * query_len] for k in range(capacity)]


def unpack(core, recv_ref, rows, both_ref, spots_ref, extra_ref, code_ref, scalar_ref, sem):
    both_ref[...] = recv_ref[...].astype(F32)[:, rows:, :]
    spots_ref[...] = jnp.where(core == 0, both_ref[:, 0, :], both_ref[:, PER_CORE, :])
    extra = jnp.where(core == 0, both_ref[:, 1, :], both_ref[:, PER_CORE + 1, :])
    extra_ref[...] = extra
    code_ref[...] = extra.astype(jnp.int32)
    return pltpu.make_async_copy(code_ref, scalar_ref, sem)


def slot_code(code_ref, d, k, query_len, queries):
    code = code_ref[d, query_len + k]
    return lax.div(code, jnp.int32(queries)), lax.rem(code, jnp.int32(queries))


def places(core, other, shape, queries):
    source = (1 - core) if other else core
    return iota(shape, 1) - queries * (source * shape[0] + iota(shape, 0))


def token_kernel(capacity, block, other, core_ref, recv_ref, emb_ref, *refs):
    if other:
        so_far_ref, near_ref, *refs = refs
    extra_ref, token_ref, exp_ref, part_ref, *refs = refs
    if other:
        kept_ref, *refs = refs
        kept_ref[0] = near_ref[...]
        kept_ref[1] = recv_ref[...]
    both_ref, spots_ref, code_ref, acc_ref, scalar_ref, sem = refs
    chips, _, emb_dim = recv_ref.shape
    queries, query_len = block
    rows = queries * query_len
    core = core_ref[0]
    copy = unpack(core, recv_ref, rows, both_ref, spots_ref, extra_ref, code_ref, scalar_ref, sem)
    copy.start()
    acc_ref[...] = jnp.zeros_like(acc_ref)
    copy.wait()
    lane = iota((query_len, WIDE), 1).astype(F32)

    spots = picked(spots_ref, extra_ref, 0, query_len, capacity, chips)
    for d in range(chips):
        for k in range(capacity):
            p, j = slot_code(scalar_ref, d, k, query_len, queries)
            mask = jnp.where(spots[k][:, d : d + 1] == lane, 1.0, 0.0).astype(BF16)
            token = jnp.dot(mask, emb_ref[p], preferred_element_type=F32)
            token_ref[d, k] = token.astype(BF16)
            start = pl.multiple_of(j * query_len, query_len)
            query = recv_ref[d, pl.ds(start, query_len), :].astype(F32)
            acc_ref[k, d : d + 1, :] = jnp.sum(token * query, axis=0, keepdims=True)
    shape = (chips, emb_dim)
    at = iota(shape, 1)
    extra = extra_ref[...]
    scores = jnp.zeros(shape, F32)
    for k in range(capacity):
        scores = jnp.where(at == k, jnp.sum(acc_ref[k], axis=-1, keepdims=True), scores)
    exps = jnp.where(at < capacity, jnp.exp(scores) * field(extra, query_len, VALID), 0.0)
    exp_ref[...] = exps
    which = field(extra, query_len, WHICH)
    place = places(core, other, shape, queries)
    total = jnp.zeros(shape, F32)
    for q in range(queries):
        share = jnp.sum(jnp.where(which == float(q), exps, 0.0), axis=1, keepdims=True)
        total = jnp.where(place == q, share, total)
    total = jnp.sum(total, axis=0, keepdims=True)
    if other:
        total = total + so_far_ref[0]
    part_ref[...] = jnp.broadcast_to(total[None], part_ref.shape)


def slot_weights(capacity, queries, query_len, neg, core, other, sums, extra, exps):
    place = places(core, other, exps.shape, queries)
    which = field(extra, query_len, WHICH)
    share = jnp.zeros_like(exps)
    for q in range(queries):
        norm = jnp.sum(jnp.where(place == q, sums, 0.0), axis=-1, keepdims=True)
        share = jnp.where(which == float(q), exps / norm, share)
    target = field(extra, query_len, HIGH) + field(extra, query_len, MID)
    target = target + field(extra, query_len, LOW)
    weights = neg * (share - target) * field(extra, query_len, VALID)
    return jnp.where(iota(exps.shape, 1) < capacity, weights, 0.0)


def weight_kernel(capacity, block, neg, other, core_ref, parts_ref, extra_ref, exp_ref, token_ref, out_ref, scale_ref):
    queries, query_len = block
    chips, emb_dim = exp_ref.shape
    extra = extra_ref[...]
    sums = jnp.sum(parts_ref[...], axis=0)
    weights = slot_weights(
        capacity, queries, query_len, neg, core_ref[0], other, sums, extra, exp_ref[...]
    )
    which = field(extra, query_len, WHICH)
    for q in range(queries):
        scale = jnp.where(which == float(q), weights, 0.0)
        for k in range(capacity):
            scale_ref[q * capacity + k] = jnp.broadcast_to(scale[:, k : k + 1], scale.shape)

    def one_device(d, carry):
        tokens = [token_ref[d, k].astype(F32) for k in range(capacity)]
        for q in range(queries):
            grad = scale_ref[q * capacity, pl.ds(d, 1), :] * tokens[0]
            for k in range(1, capacity):
                grad = grad + scale_ref[q * capacity + k, pl.ds(d, 1), :] * tokens[k]
            out_ref[d, q * query_len : (q + 1) * query_len, :] = grad.astype(BF16)
        return carry

    lax.fori_loop(0, chips, one_device, 0, unroll=8)


def add_kernel(left_ref, right_ref, out_ref):
    out_ref[...] = (left_ref[...].astype(F32) + right_ref[...].astype(F32)).astype(BF16)


def passage_kernel(capacity, block, neg, core_ref, hidden_ref, unit_ref, inverse_ref, parts_ref, *refs):
    kept_ref, *refs = refs
    halves = [(kept_ref.at[h], refs[h]) for h in range(CORES)]
    grad_ref, term_ref, table_ref, total_ref, weight_ref, *refs = refs[CORES:]
    order_ref, unit_own_ref, inverse_own_ref, own_sem, *refs = refs
    loads = []
    for n, (source, target) in enumerate(
        ((unit_ref, unit_own_ref), (inverse_ref, inverse_own_ref))
    ):
        loads.append(pltpu.make_async_copy(source, target, own_sem.at[n]))
        loads[n].start()
    passes, pass_len, _ = hidden_ref.shape
    emb_dim = unit_ref.shape[2]
    queries, query_len = block
    rows = queries * query_len
    lane = iota((query_len, WIDE), 1).astype(F32)
    copies = []
    for half, (recv_ref, _) in enumerate(halves):
        copy = unpack(core_ref[0], recv_ref, rows, *[ref.at[half] for ref in refs])
        copy.start()
        copies.append(copy)
    _, spots_ref, extra_ref, _, scalar_ref, _ = refs
    total_ref[...] = jnp.zeros_like(total_ref)
    table_ref[...] = jnp.zeros_like(table_ref)
    sums = jnp.sum(parts_ref[...], axis=0)
    for half, (recv_ref, exp_ref) in enumerate(halves):
        weights = slot_weights(
            capacity,
            queries,
            query_len,
            neg,
            core_ref[0],
            half == 1,
            sums,
            extra_ref[half],
            exp_ref[...],
        )
        for k in range(capacity):
            weight_ref[half, k] = jnp.broadcast_to(weights[:, k : k + 1], weights.shape)
    for half, (recv_ref, _) in enumerate(halves):
        chips = recv_ref.shape[0]
        copies[half].wait()

        def one_group(group, carry):
            spots = picked(spots_ref.at[half], extra_ref.at[half], group, query_len, capacity)

            def place(step, k):
                d = group * GROUP + step
                p, j = slot_code(scalar_ref.at[half], d, k, query_len, queries)
                return d, p, pl.multiple_of(step * rows + j * query_len, query_len)

            table_ref[...] = jnp.zeros_like(table_ref)
            for step in range(GROUP):
                for k in range(capacity):
                    d, p, start = place(step, k)
                    weight = weight_ref[half, k, pl.ds(d, 1), :]
                    weight = jnp.concatenate([weight] * (WIDE // emb_dim), axis=1)
                    added = jnp.where(spots[k][:, step : step + 1] == lane, weight, 0.0).astype(BF16)
                    table_ref[p, pl.ds(start, query_len), :] = (
                        table_ref[p, pl.ds(start, query_len), :] + added
                    )
            left = recv_ref[pl.ds(group * GROUP, GROUP), :rows, :].reshape(GROUP * rows, emb_dim)
            left = left.T
            for p in range(passes):
                total_ref[p] = total_ref[p] + jnp.dot(
                    left, table_ref[p], preferred_element_type=F32
                )
            return carry

        for group in range(chips // GROUP):
            one_group(group, 0)
    for load in loads:
        load.wait()
    term = jnp.zeros(term_ref.shape, F32)
    for p in range(passes):
        unit = unit_own_ref[p][:pass_len]
        grad = total_ref[p].T[:pass_len]
        grad = grad - unit * jnp.sum(unit * grad, axis=-1, keepdims=True)
        raw_grad = (grad * inverse_own_ref[p][:pass_len]).astype(BF16)
        order_ref[:, p, :] = raw_grad.astype(F32)
        term = term + lax.dot_general(
            raw_grad, hidden_ref[p], (((0,), (0,)), ((), ())), preferred_element_type=F32
        )
    term_ref[...] = term
    grad_ref[...] = order_ref[...].astype(BF16)


def copy_kernel(from_ref, to_ref):
    to_ref[...] = from_ref[...]


def query_kernel(parts_ref, query_ref, proj_ref, term_ref, out_ref):
    hidden = query_ref[...]
    unit, length = unit_rows(jnp.dot(hidden, proj_ref[...], preferred_element_type=F32))
    grad = jnp.sum(parts_ref[...].astype(F32), axis=0)
    raw_grad = unit_back(grad, unit, length).astype(BF16)
    term = lax.dot_general(
        raw_grad, hidden, (((0,), (0,)), ((), ())), preferred_element_type=F32
    )
    term = term + term_ref[...]
    out_ref[...] = term.T.reshape(out_ref.shape).astype(BF16)


def swap(array, axes):
    return lax.all_to_all(array, axes, split_axis=0, concat_axis=0, tiled=True)


def to_other_core(array):
    return lax.ppermute(array, "core", [(c, CORES - 1 - c) for c in range(CORES)])


def per_device(query_hidden, passage_hidden, projection, negatives, positions, teacher):
    query_count, query_len, hidden_dim = query_hidden.shape
    pass_count, pass_len, _ = passage_hidden.shape
    emb_dim = projection.shape[1]
    neg_count = negatives.shape[1]
    chips = lax.axis_size("x") * lax.axis_size("z")
    owners = chips * CORES
    reps = lax.axis_size("rep")
    pair_count = query_count * neg_count
    capacity = (pair_count + owners - 2) // (owners - 1)
    rows = query_count * query_len
    block = (query_count, query_len)
    query_flat = query_hidden.reshape(rows, hidden_dim)
    core = lax.axis_index("core").reshape(1)

    def call(kernel, outs, scratch, *args, scalars=(), streamed=(), mb=16):
        results = pl.pallas_call(
            kernel,
            out_shape=outs,
            in_specs=[
                SMEM if n in scalars else pl.BlockSpec(memory_space=pl.ANY) if n in streamed else VMEM
                for n in range(len(args))
            ],
            out_specs=[VMEM] * len(outs),
            scratch_shapes=scratch,
            compiler_params=params(mb),
        )(*args)
        return results[0] if len(outs) == 1 else results

    shape = jax.ShapeDtypeStruct
    slot_shape = (chips, emb_dim)
    meta_shape = (chips, META_ROWS, emb_dim)
    recv_shape = (chips, rows + META_ROWS, emb_dim)
    send = call(
        lambda *refs: request_kernel(reps, pass_count, *refs),
        [shape(recv_shape, BF16)],
        [pltpu.VMEM(meta_shape, F32)],
        query_flat,
        projection,
        negatives,
        jnp.swapaxes(positions, 1, 2),
        teacher,
        mb=56,
    )
    near = swap(send, ("x", "z"))
    wide_shape = (pass_count, WIDE, emb_dim)
    emb, unit, inverse = call(
        embed_kernel,
        [shape(wide_shape, BF16), shape(wide_shape, F32), shape(wide_shape, F32)],
        [],
        passage_hidden,
        projection,
    )
    near, emb = lax.optimization_barrier((near, emb))
    far = to_other_core(near)
    halves = []
    so_far = []
    for other, recv in ((False, near), (True, far)):
        extra, tokens, exps, part, *kept = call(
            lambda *refs: token_kernel(capacity, block, other, *refs),
            [
                shape(slot_shape, F32),
                shape((chips, capacity, query_len, emb_dim), BF16),
                shape(slot_shape, F32),
                shape((owners if other else 1, 1, emb_dim), F32),
            ]
            + [shape((CORES,) + recv_shape, BF16)] * other,
            [
                pltpu.VMEM(meta_shape, F32),
                pltpu.VMEM(slot_shape, F32),
                pltpu.VMEM(slot_shape, jnp.int32),
                pltpu.VMEM((capacity,) + slot_shape, F32),
                pltpu.SMEM(slot_shape, jnp.int32),
                pltpu.SemaphoreType.DMA,
            ],
            core,
            recv,
            emb,
            *so_far,
            scalars=(0,),
        )
        so_far = [part, near]
        halves.append((extra, exps, tokens))
    parts = swap(part, ("x", "z", "core"))

    def weigh(other):
        extra, exps, tokens = halves[other]
        return call(
            lambda *refs: weight_kernel(capacity, block, neg_count, other, *refs),
            [shape((chips, rows, emb_dim), BF16)],
            [
                pltpu.VMEM((query_count * capacity,) + slot_shape, F32),
            ],
            core,
            parts,
            extra,
            exps,
            tokens,
            scalars=(0,),
        )

    far_part = to_other_core(weigh(True))
    near_part = weigh(False)
    query_parts = call(add_kernel, [shape(near_part.shape, BF16)], [], near_part, far_part)
    query_parts, sums = lax.optimization_barrier((query_parts, parts))
    query_parts = swap(query_parts, ("x", "z"))
    grad_passages, term = call(
        lambda *refs: passage_kernel(capacity, block, neg_count, *refs),
        [
            shape((pass_len, pass_count, emb_dim), BF16),
            shape((emb_dim, hidden_dim), F32),
        ],
        [
            pltpu.VMEM((pass_count, GROUP * rows, WIDE), BF16),
            pltpu.VMEM((pass_count, emb_dim, WIDE), F32),
        ]
        + [
            pltpu.VMEM((CORES, capacity) + slot_shape, F32),
            pltpu.VMEM((pass_len, pass_count, emb_dim), F32),
            pltpu.VMEM(wide_shape, F32),
            pltpu.VMEM(wide_shape, F32),
            pltpu.SemaphoreType.DMA((2,)),
            pltpu.VMEM((CORES,) + meta_shape, F32),
            pltpu.VMEM((CORES,) + slot_shape, F32),
            pltpu.VMEM((CORES,) + slot_shape, F32),
            pltpu.VMEM((CORES,) + slot_shape, jnp.int32),
            pltpu.SMEM((CORES,) + slot_shape, jnp.int32),
            pltpu.SemaphoreType.DMA((CORES,)),
        ],
        core,
        passage_hidden,
        unit,
        inverse,
        sums,
        kept[0],
        halves[0][1],
        halves[1][1],
        scalars=(0,),
        streamed=(2, 3),
        mb=56,
    )
    term = call(copy_kernel, [shape(term.shape, F32)], [], term, mb=8)
    groups = lax.axis_size(("x", "core", "rep"))
    pieces = call(
        query_kernel,
        [shape((groups, hidden_dim // groups, emb_dim), BF16)],
        [],
        query_parts,
        query_flat,
        projection,
        term,
        mb=16,
    )
    pieces = swap(pieces, ("x", "core", "rep"))
    mine = jnp.sum(pieces.astype(F32), axis=0).astype(BF16)
    copies = swap(jnp.broadcast_to(mine[None], (lax.axis_size("z"),) + mine.shape), "z")
    scale = 1.0 / math.sqrt(owners * reps * (query_count * query_len + pass_count * pass_len))
    mine = (jnp.sum(copies.astype(F32), axis=0) * scale).astype(BF16)
    copies = swap(jnp.broadcast_to(mine[None], (groups,) + mine.shape), ("x", "core", "rep"))
    grad_passages = jnp.swapaxes(grad_passages, 0, 1)
    return (grad_passages, copies.reshape(hidden_dim, emb_dim).astype(F32))


def solution(mesh):
    devices = mesh.devices.reshape(CHIPS_X, -1, CORES, mesh.shape["rep"])
    mesh = Mesh(devices, ("x", "z", "core", "rep"))
    whole = ("x", "z", "core", "rep")
    in_specs = (
        P(whole, None, None),
        P(whole, None, None),
        P(),
        P(whole, None),
        P(whole, None, None),
        P(whole, None),
    )
    out_specs = (P(whole, None, None), P())
    return jax.shard_map(
        per_device, mesh=mesh, in_specs=in_specs, out_specs=out_specs, check_vma=False
    )
```
